1024 devices in a mesh: dp: 64 (over z, y), expert: 16 (over x, core).
Axes of the slice: x: 8, y: 8, z: 8, core: 2. Of those that a mesh axis runs over, the one named last changes fastest.
Arguments:
- tokens: bfloat16 [131072, 1024], P(('dp', 'expert')), may hold values from -6 to 6
- route_ids: int32 [131072, 1], P(('dp', 'expert')), may hold values from 0 to 15; in each aligned block of 128 rows (0 to 127, 128 to 255, ...) at most 12 rows name the same one
- route_weight: float32 [131072, 1], P(('dp', 'expert')), may hold values from 0.02 to 0.5
- w_gate_up: bfloat16 [16, 1024, 768], P('expert'), may hold values from -0.1875 to 0.1875
- w_down: bfloat16 [16, 384, 1024], P('expert'), may hold values from -0.3125 to 0.3125
- out_grad: bfloat16 [131072, 1024], P(('dp', 'expert')), may hold values from -6 to 6
Outputs:
- mixed: bfloat16 [131072, 1024], P(('dp', 'expert'))
- token_grad: bfloat16 [131072, 1024], P(('dp', 'expert'))
- route_weight_grad: float32 [131072, 1], P(('dp', 'expert'))
- weight_grad: float32 [16, 1024, 1152], P('expert', 'dp')
The draws below stay inside these ranges and needn't reach their ends.
Inputs may be any that keep to these rules, and one draw needn't show every extreme that they name: `route_ids`: among the 128 rows of one device (aligned blocks), no expert is named by more than 12 rows, a bound that some block reaches; a row names 1 different experts.
All inputs are finite; a program needn't handle non-finite values.
Results may differ from the reference program's by a relative error of at most 0.0057.
Values may be sent and summed in bfloat16 or wider, within the bound.
A program may use at most 32 MiB of HBM per device.

```python
import math
import jax
import jax.numpy as jnp
import numpy as np
from jax import lax

D = 1024
H = 384
TOK_DEV = 128
TOPK = 1
EXPERTS = 16
CAP = 12
TOKENS = 131072


def shard_levels(stream_key, dims, split, least, high):
    def one(axis_at, parts):
        steps = jax.random.uniform(jax.random.fold_in(jax.random.fold_in(stream_key, 6), axis_at), (parts,), jnp.float32, least / len(split), high / len(split))
        return jnp.repeat(jnp.exp(steps), dims[axis_at] // parts).reshape((-1,) + (1,) * (len(dims) - axis_at - 1))

    gain = one(*split[0])
    for cut in split[1:]:
        gain = gain * one(*cut)
    return gain


def assign_block(own_key, own, number, rows, amount, top, limit, slope):
    sequence = jax.random.permutation(own_key, amount)
    packed, usual = load_shares(amount, rows * top, limit, slope, True), load_shares(amount, rows * top, limit, slope, False)
    places = jnp.arange(amount)

    def named(sizes, turn):
        used = int((sizes > 0).sum())
        fixed = max(1, used // 4)
        shifted = fixed + (places - fixed + turn * (used - fixed)) % max(1, amount - fixed)
        return jnp.zeros((amount,), jnp.int32).at[sequence[jnp.where(places < fixed, places, shifted)]].set(jnp.asarray(sizes, jnp.int32))

    sizes = jnp.where(number % 4 == 0, named(packed, number // 4), named(usual, number - number // 4 - 1))
    mixed = jax.random.permutation(jax.random.fold_in(own, 3), amount)
    giver, sink = mixed[0:amount // 2 * 2:2], mixed[1:amount // 2 * 2:2]
    slack = jnp.minimum(sizes[giver] - 1, limit - sizes[sink]) // 2
    slack = jnp.where((giver == sequence[0]) | (sink == sequence[0]) | (sizes[sink] == 0), 0, jnp.maximum(slack, 0))
    shifted = jax.random.randint(jax.random.fold_in(own, 4), (amount // 2,), 0, 1 << 20) % (slack + 1)
    sizes = sizes.at[giver].add(-shifted).at[sink].add(shifted)
    labels = jnp.searchsorted(jnp.cumsum(sizes), jnp.arange(rows * top), side="right").astype(jnp.int32)
    table = labels.reshape(top, rows).T
    table = table[jax.random.permutation(jax.random.fold_in(own, 1), rows)]
    turn = jax.random.randint(jax.random.fold_in(own, 2), (rows, 1), 0, top)
    return jnp.take_along_axis(table, (jnp.arange(top)[None, :] + turn) % top, axis=1)


def load_shares(count, total, limit, lean, full):
    loads = [(1 << 20) // math.isqrt(standing ** lean) + 1 for standing in range(1, count + 1)]
    largest = limit if full else min(limit, max(-(-total // count), total * loads[0] // sum(loads)))
    least = 1 if total - largest >= count - 1 else 0
    given, rest = [largest] + [least] * (count - 1), total - largest - least * (count - 1)
    while rest > 0:
        movable = [i for i in range(1, count) if given[i] < largest] or [i for i in range(1, count) if given[i] < limit]
        mass, budget = sum([loads[i] for i in movable]), rest
        for i in movable:
            extra = min(limit - given[i], max(1, budget * loads[i] // mass), rest)
            given[i] = given[i] + extra
            rest = rest - extra
    return np.array(given)


def scatter_about(own_key, extent, scale, most, split=(), kind=jnp.bfloat16):
    loudness = shard_levels(own_key, extent, split, -0.22, 0.18) if split else 1.0
    values = jax.random.normal(own_key, extent, jnp.float32) * scale * loudness
    return jnp.minimum(jnp.maximum(values, -most), most).astype(kind)


def setup_inputs(seed: int = 0) -> dict:
    key_of = jax.random.split(jax.random.key(seed), 7)
    tokens = scatter_about(key_of[0], (TOKENS, D), 1.0, 6.0, ((0, 1024),))
    route_ids_keys = jax.random.split(jax.random.fold_in(key_of[1], 1), TOKENS // TOK_DEV)
    route_ids_turns = jax.random.permutation(jax.random.fold_in(key_of[1], 3), TOKENS // TOK_DEV)
    route_ids = jax.vmap(lambda own, number: assign_block(jax.random.fold_in(key_of[1], 2), own, number, TOK_DEV, EXPERTS, TOPK, CAP, 2))(route_ids_keys, route_ids_turns).reshape((TOKENS, TOPK))
    route_weight = jnp.clip(jnp.exp(math.log(0.5) - 3.218876 * jax.random.uniform(key_of[2], (TOKENS, TOPK), jnp.float32) ** shard_levels(key_of[2], (TOKENS, TOPK), ((0, 1024),), -0.2, 0.2)), 0.02, 0.5)
    w_gate_up = scatter_about(key_of[3], (EXPERTS, D, 2 * H), D ** -0.5, 0.1875, ((0, 16),))
    w_down = scatter_about(key_of[4], (EXPERTS, H, D), H ** -0.5, 0.3125, ((0, 16),))
    out_grad = scatter_about(key_of[5], (TOKENS, D), 1.0, 6.0, ((0, 1024),))
    return dict(tokens=tokens, route_ids=route_ids, route_weight=route_weight, w_gate_up=w_gate_up, w_down=w_down, out_grad=out_grad)


def reference(tokens, route_ids, route_weight, w_gate_up, w_down, out_grad):
    count = tokens.shape[0]
    width = tokens.shape[1]
    hidden = w_down.shape[1]
    blocks = count // TOK_DEV
    per_block = TOK_DEV * TOPK
    ids = route_ids.reshape(blocks, per_block)
    onehot = (ids[:, :, None] == jnp.arange(EXPERTS, dtype=jnp.int32)[None, None, :]).astype(jnp.int32)
    position = jnp.sum((jnp.cumsum(onehot, axis=1) - onehot) * onehot, axis=2).astype(jnp.int32)
    copy_index = (jnp.arange(blocks, dtype=jnp.int32)[:, None] * per_block
                  + jnp.arange(per_block, dtype=jnp.int32)[None, :]).astype(jnp.int32)
    table = jnp.full((EXPERTS, blocks, CAP), count * TOPK, jnp.int32)
    block_rows = jnp.broadcast_to(jnp.arange(blocks, dtype=jnp.int32)[:, None], (blocks, per_block))
    table = table.at[ids, block_rows, position].set(copy_index)
    token_pad = jnp.concatenate([tokens, jnp.zeros((1, width), tokens.dtype)], axis=0)
    grad_pad = jnp.concatenate([out_grad, jnp.zeros((1, width), out_grad.dtype)], axis=0)
    weight_pad = jnp.concatenate([route_weight.reshape(-1), jnp.zeros((1,), jnp.float32)], axis=0)

    def per_expert(carry, inputs):
        mixed_sum, dx_sum, route_sum = carry
        slots, gate_up, down = inputs
        flat = slots.reshape(-1)
        source = (flat // TOPK).astype(jnp.int32)
        rows = token_pad[source]
        pre = jnp.dot(rows, gate_up, preferred_element_type=jnp.float32)
        gate_pre = pre[:, :hidden]
        up_pre = pre[:, hidden:]
        sig = jax.nn.sigmoid(gate_pre)
        silu_gate = gate_pre * sig
        act = (silu_gate * up_pre).astype(jnp.bfloat16)
        result = jnp.dot(act, down, preferred_element_type=jnp.float32).astype(jnp.bfloat16)
        result_f = result.astype(jnp.float32)
        scale = weight_pad[flat]
        mixed_sum = mixed_sum.at[source].add(scale[:, None] * result_f)
        upstream = grad_pad[source].astype(jnp.float32)
        route_sum = route_sum.at[flat].add(jnp.sum(upstream * result_f, axis=1))
        cotan = (scale[:, None] * upstream).astype(jnp.bfloat16)
        d_act = jnp.dot(cotan, down.T, preferred_element_type=jnp.float32)
        d_gate = d_act * up_pre * sig * (1.0 + gate_pre * (1.0 - sig))
        d_up = d_act * silu_gate
        d_pre = jnp.concatenate([d_gate, d_up], axis=1).astype(jnp.bfloat16)
        dx_rows = jnp.dot(d_pre, gate_up.T, preferred_element_type=jnp.float32).astype(jnp.bfloat16)
        dx_sum = dx_sum.at[source].add(dx_rows.astype(jnp.float32))
        grad_gu = jnp.dot(rows.T, d_pre, preferred_element_type=jnp.float32)
        grad_down = jnp.dot(cotan.T, act, preferred_element_type=jnp.float32)
        return (mixed_sum, dx_sum, route_sum), jnp.concatenate([grad_gu, grad_down], axis=1)

    init = (jnp.zeros((count + 1, width), jnp.float32), jnp.zeros((count + 1, width), jnp.float32),
            jnp.zeros((count * TOPK + 1,), jnp.float32))
    final, grads = lax.scan(per_expert, init, (table, w_gate_up, w_down))
    mixed_sum, dx_sum, route_sum = final
    return (mixed_sum[:count].astype(jnp.bfloat16), dx_sum[:count].astype(jnp.bfloat16),
            route_sum[:count * TOPK].reshape(count, TOPK), grads)
```

```python
import functools

import jax
import jax.numpy as jnp
from jax import lax
from jax.experimental import pallas as pl
from jax.experimental.pallas import tpu as pltpu
from jax.sharding import PartitionSpec as P

MESH = pl.DeviceIdType.MESH
BF16, F32, I32 = jnp.bfloat16, jnp.float32, jnp.int32
CAP = 12
BLOCKS = 4
CUT = 256
MSG = CAP * BLOCKS
GROUP = 4 * MSG
CHIPS = (0, 1, 7, 2, 6, 3, 5, 4)
PLACE = {k: i for i, k in enumerate(CHIPS)}
FAR_FIRST = (14, 15, 12, 13, 10, 11, 8, 9, 6, 7, 4, 5, 2, 3, 1)
NT = (((1,), (1,)), ((), ()))
TN = (((0,), (0,)), ((), ()))


def mirror(slot):
    return 2 * PLACE[(8 - CHIPS[slot // 2]) % 8] + slot % 2


def rows(at, n):
    return pl.ds(at * n, n)


def dot(a, b, dims=(((1,), (0,)), ((), ()))):
    return lax.dot_general(a, b, dims, preferred_element_type=F32)


def kernel(
    ids_ref, wt_ref, tok_hbm, grad_hbm, gu_hbm, down_hbm,
    mixed_ref, tgrad_ref, rwg_ref, wgrad_ref,
    tok, grad, gu, down, spread, gather, perm,
    snd_t, snd_g, rcv_t, rcv_g, xs, gs, p1, p2, act, dpre,
    out_r, out_d, ret_r, ret_d, part, own, got,
    ld_sem, t_ss, t_rs, g_ss, g_rs, r_ss, r_rs, d_ss, d_rs,
    ft_ss, ft_rs, fg_ss, fg_rs, w_ss, w_rs,
):
    dp, ex = lax.axis_index("dp"), lax.axis_index("expert")
    y, z = lax.rem(dp, 8), lax.div(dp, 8)
    x, core = lax.div(ex, 2), lax.rem(ex, 2)

    def expert_at(slot):
        chip = lax.rem(x + CHIPS[slot // 2], 8)
        return {"expert": chip * 2 + (core if slot % 2 == 0 else 1 - core)}

    def dp_at(yy, zz):
        return {"dp": zz * 8 + yy}

    y0, z0 = y + 1 - 2 * lax.rem(y, 2), z + 1 - 2 * lax.rem(z, 2)
    y1, z1 = lax.rem(y + 7 + 2 * lax.rem(y, 2), 8), lax.rem(z + 7 + 2 * lax.rem(z, 2), 8)
    quads = (
        (dp_at(y0, z), dp_at(y, z0), dp_at(y0, z0)),
        (dp_at(y1, z), dp_at(y, z1), dp_at(y1, z1)),
    )

    def peer(m):
        return lax.rem(y + 2 * (m % 4), 8), lax.rem(z + 2 * (m // 4), 8)

    loads = []
    for b in range(BLOCKS):
        loads.append(pltpu.make_async_copy(tok_hbm.at[:, rows(b, CUT)], tok.at[rows(b, 128)], ld_sem.at[b]))
    for b in range(BLOCKS):
        loads.append(pltpu.make_async_copy(grad_hbm.at[:, rows(b, CUT)], grad.at[rows(b, 128)], ld_sem.at[4 + b]))
    loads.append(pltpu.make_async_copy(gu_hbm.at[0], gu, ld_sem.at[8]))
    loads.append(pltpu.make_async_copy(down_hbm.at[0], down, ld_sem.at[9]))

    barrier = pltpu.get_barrier_semaphore()
    for m in (10, 9, 11, 6, 14, 5, 7, 13, 15, 8, 2, 1, 3, 4, 12):
        pl.semaphore_signal(barrier, 1, device_id=dp_at(*peer(m)), device_id_type=MESH)
    for slot in FAR_FIRST:
        pl.semaphore_signal(barrier, 1, device_id=expert_at(slot), device_id_type=MESH)
    for quad in quads:
        for device in quad:
            pl.semaphore_signal(barrier, 1, device_id=device, device_id_type=MESH)
    for load in loads:
        load.start()

    sub = lax.broadcasted_iota(I32, (128, 128), 0)
    lane = lax.broadcasted_iota(I32, (128, 128), 1)
    eye = sub == lane

    def column(row):
        return jnp.sum(jnp.where(eye, row, 0.0), axis=1, keepdims=True)

    ids = ids_ref[...]
    chip = ((ids >> 1) + (8 - x)) & 7
    place = jnp.where(chip > 4, 16 - 2 * chip, jnp.where(chip == 0, 0, 2 * chip - 1))
    slot_row = (2 * place + ((ids + core) & 1)).astype(F32)
    slot_col = column(slot_row)
    same = slot_row == slot_col
    before_row = jnp.sum(jnp.where(same & (sub < lane), 1.0, 0.0), axis=0, keepdims=True)
    before_col = jnp.sum(jnp.where(same & (lane < sub), 1.0, 0.0), axis=1, keepdims=True)
    at_row = (slot_row * float(MSG) + before_row).astype(I32)
    at_col = (slot_col * float(MSG) + before_col).astype(I32)
    weight = column(wt_ref[...])

    down_rows = lax.broadcasted_iota(I32, (16 * MSG, 128), 0)
    for b in range(BLOCKS):
        spread[:, b * 128:(b + 1) * 128] = jnp.where(down_rows == at_row + CAP * b, 1.0, 0.0).astype(BF16)
    for b in range(BLOCKS):
        loads[b].wait()
    snd_t[...] = dot(spread[...], tok[...]).astype(BF16)

    pl.semaphore_wait(barrier, 36)

    def exchange(slot, src, dst, ss, rs):
        other = mirror(slot)
        return pltpu.make_async_remote_copy(
            src.at[rows(slot, MSG)], dst.at[rows(other, MSG)], ss.at[slot], rs.at[other],
            device_id=expert_at(slot), device_id_type=MESH,
        )

    def arrival(slot, src, dst, ss, rs):
        return pltpu.make_async_remote_copy(
            src.at[rows(slot, MSG)], dst.at[rows(slot, MSG)], ss.at[slot], rs.at[slot],
            device_id=expert_at(slot), device_id_type=MESH,
        )

    tset, gset = (snd_t, rcv_t, t_ss, t_rs), (snd_g, rcv_g, g_ss, g_rs)
    rset, dset = (out_r, ret_r, r_ss, r_rs), (out_d, ret_d, d_ss, d_rs)
    for slot in FAR_FIRST:
        exchange(slot, *tset).start()
    for b in range(BLOCKS):
        loads[4 + b].wait()
    for b in range(BLOCKS):
        grad_b = grad[rows(b, 128), :].astype(F32)
        tok[rows(b, 128), :] = (weight * grad_b).astype(BF16)
    snd_g[...] = dot(spread[...], tok[...]).astype(BF16)
    for slot in FAR_FIRST:
        exchange(slot, *gset).start()
    rcv_t[0:MSG, :] = snd_t[0:MSG, :]
    rcv_g[0:MSG, :] = snd_g[0:MSG, :]

    up = lax.broadcasted_iota(I32, (GROUP, GROUP), 0)
    across = lax.broadcasted_iota(I32, (GROUP, GROUP), 1)
    twelfth = (up * 5462) >> 16
    target = (twelfth & 3) * MSG + (twelfth >> 2) * CAP + (up - twelfth * CAP)
    perm[...] = jnp.where(across == target, 1.0, 0.0).astype(BF16)

    def forward(group, m, buf, ss, rs):
        return pltpu.make_async_remote_copy(
            buf.at[rows(4 * group, MSG)], buf.at[rows(4 * group + m, MSG)],
            ss.at[4 * group + m], rs.at[4 * group + m],
            device_id=quads[group // 2][m - 1], device_id_type=MESH,
        )

    ftset, fgset = (xs, ft_ss, ft_rs), (gs, fg_ss, fg_rs)

    def take(group, kind, fkind):
        buf = fkind[0]
        for slot in range(4 * group, 4 * group + 4):
            if slot:
                arrival(slot, *kind).wait_recv()
        turned = dot(perm[...], kind[1][rows(group, GROUP), :]).astype(BF16)
        for b in range(BLOCKS):
            buf[rows(4 * group, MSG), b * CUT:(b + 1) * CUT] = turned[b * MSG:(b + 1) * MSG, :]
        for m in (3, 2, 1):
            forward(group, m, *fkind).start()

    def give(group, value, kind):
        buf = kind[0]
        stacked = jnp.concatenate([value[:, b * CUT:(b + 1) * CUT] for b in range(BLOCKS)], axis=0)
        buf[rows(group, GROUP), :] = dot(perm[...], stacked).astype(BF16)
        for slot in range(4 * group, 4 * group + 4):
            if slot:
                exchange(slot, *kind).start()

    order = (3, 2, 1, 0)
    for group in order:
        take(group, tset, ftset)
    loads[8].wait()
    loads[9].wait()
    for group in order:
        for m in (1, 2, 3):
            forward(group, m, *ftset).wait_recv()
        pre = dot(xs[rows(group, GROUP), :], gu[...])
        a, u = pre[:, :384], pre[:, 384:]
        s = 1.0 / (1.0 + jnp.exp(-a))
        silu = a * s
        act[rows(group, GROUP), :] = (silu * u).astype(BF16)
        p1[rows(group, GROUP), :] = u * s * (1.0 + a * (1.0 - s))
        p2[rows(group, GROUP), :] = silu
    for b in range(BLOCKS):
        right = lax.broadcasted_iota(I32, (128, 16 * MSG), 1)
        gather[rows(b, 128), :] = jnp.where(right == at_col + CAP * b, 1.0, 0.0).astype(BF16)
    for group in order:
        take(group, gset, fgset)
    for group in order:
        result = dot(act[rows(4 * group, MSG), :], down[...]).astype(BF16)
        give(group, result, rset)
    for group in order:
        for m in (1, 2, 3):
            forward(group, m, *fgset).wait_recv()
        d_act = dot(gs[rows(group, GROUP), :], down[...], NT)
        dpre[rows(group, GROUP), 0:384] = (d_act * p1[rows(group, GROUP), :]).astype(BF16)
        dpre[rows(group, GROUP), 384:768] = (d_act * p2[rows(group, GROUP), :]).astype(BF16)

    def share(m):
        yy, zz = peer(m)
        other = ((4 - m // 4) % 4) * 4 + (4 - m % 4) % 4
        return pltpu.make_async_remote_copy(
            part.at[m // 4, yy], got.at[other], w_ss.at[m], w_rs.at[other],
            device_id=dp_at(yy, zz), device_id_type=MESH,
        )

    def shared(m):
        return pltpu.make_async_remote_copy(
            part.at[m // 4, y], got.at[m], w_ss.at[m], w_rs.at[m],
            device_id=dp_at(*peer(m)), device_id_type=MESH,
        )

    for i in (2, 1, 3, 0):
        tile = pl.ds(pl.multiple_of(lax.rem(z + 2 * i, 8) * 128, 128), 128)
        first = dot(xs[:, tile], dpre[...], TN)
        last = dot(gs[:, tile], act[...], TN)
        for j in range(8):
            part[i, j, :, 0:768] = first[j * 16:(j + 1) * 16, :].astype(BF16)
            part[i, j, :, 768:1152] = last[j * 16:(j + 1) * 16, :].astype(BF16)
            if i == 0:
                own[j, :, 0:768] = first[j * 16:(j + 1) * 16, :]
                own[j, :, 768:1152] = last[j * 16:(j + 1) * 16, :]
        for j in (2, 1, 3, 0):
            if i or j:
                share(4 * i + j).start()

    for group in order:
        dx = dot(dpre[rows(4 * group, MSG), :], gu[...], NT).astype(BF16)
        give(group, dx, dset)
    ret_r[0:MSG, :] = out_r[0:MSG, :]
    ret_d[0:MSG, :] = out_d[0:MSG, :]

    for slot in range(1, 16):
        arrival(slot, *rset).wait_recv()
    inner = jnp.zeros((128, 1), F32)
    for b in range(BLOCKS):
        copy_out = dot(gather[rows(b, 128), :], ret_r[...])
        mixed_ref[:, b * CUT:(b + 1) * CUT] = (weight * copy_out).astype(BF16)
        inner = inner + jnp.sum(grad[rows(b, 128), :].astype(F32) * copy_out, axis=1, keepdims=True)
    rwg_ref[...] = jnp.sum(jnp.where(eye, inner, 0.0), axis=0, keepdims=True)
    for slot in range(1, 16):
        arrival(slot, *dset).wait_recv()
    for b in range(BLOCKS):
        tgrad_ref[:, b * CUT:(b + 1) * CUT] = dot(gather[rows(b, 128), :], ret_d[...]).astype(BF16)

    total = own[y]
    for m in range(1, 16):
        shared(m).wait_recv()
        total = total + got[m].astype(F32)
    wgrad_ref[0] = total

    for slot in range(1, 16):
        for kind in (tset, gset, rset, dset):
            exchange(slot, *kind).wait_send()
        share(slot).wait_send()
    for group in range(4):
        for m in (1, 2, 3):
            for kind in (ftset, fgset):
                forward(group, m, *kind).wait_send()


def on_device(tokens, route_ids, route_weight, w_gate_up, w_down, out_grad):
    count, width = tokens.shape
    hidden = w_down.shape[1]
    dma = pltpu.SemaphoreType.DMA
    vmem = pl.BlockSpec(memory_space=pltpu.VMEM)
    hbm = pl.BlockSpec(memory_space=pl.ANY)
    slots = 16 * MSG
    scratch = [
        pltpu.VMEM((512, CUT), BF16), pltpu.VMEM((512, CUT), BF16),
        pltpu.VMEM((width, 2 * hidden), BF16), pltpu.VMEM((hidden, width), BF16),
        pltpu.VMEM((slots, 512), BF16), pltpu.VMEM((512, slots), BF16), pltpu.VMEM((GROUP, GROUP), BF16),
        *[pltpu.VMEM((slots, CUT), BF16)] * 4,
        pltpu.VMEM((slots, width), BF16), pltpu.VMEM((slots, width), BF16),
        pltpu.VMEM((slots, hidden), F32), pltpu.VMEM((slots, hidden), F32),
        pltpu.VMEM((slots, hidden), BF16), pltpu.VMEM((slots, 2 * hidden), BF16),
        *[pltpu.VMEM((slots, CUT), BF16)] * 4,
        pltpu.VMEM((4, 8, 16, 3 * hidden), BF16), pltpu.VMEM((8, 16, 3 * hidden), F32),
        pltpu.VMEM((16, 16, 3 * hidden), BF16),
        dma((10,)), *[dma((16,))] * 14,
    ]
    mixed, tgrad, rwg, wgrad = pl.pallas_call(
        kernel,
        out_shape=(
            jax.ShapeDtypeStruct((count, width), BF16),
            jax.ShapeDtypeStruct((count, width), BF16),
            jax.ShapeDtypeStruct((1, count), F32),
            jax.ShapeDtypeStruct((1, 16, 3 * hidden), F32),
        ),
        in_specs=[vmem, vmem, hbm, hbm, hbm, hbm],
        out_specs=[vmem] * 4,
        scratch_shapes=scratch,
        compiler_params=pltpu.CompilerParams(
            collective_id=0, has_side_effects=True, vmem_limit_bytes=48 * 2**20
        ),
    )(route_ids.reshape(1, count), route_weight.reshape(1, count), tokens, out_grad, w_gate_up, w_down)
    return mixed, tgrad, rwg.reshape(count, 1), wgrad


def solution(mesh):
    rows_split = P(("dp", "expert"), None)
    return jax.shard_map(
        on_device,
        mesh=mesh,
        in_specs=(rows_split, rows_split, rows_split, P("expert", None, None), P("expert", None, None), rows_split),
        out_specs=(rows_split, rows_split, rows_split, P("expert", "dp", None)),
        check_vma=False,
    )
```

```python
import jax
import jax.numpy as jnp
from jax import lax
from jax.experimental import pallas as pl
from jax.experimental.pallas import tpu as pltpu
from jax.sharding import PartitionSpec as P

MESH = pl.DeviceIdType.MESH
BF16, F32, I32 = jnp.bfloat16, jnp.float32, jnp.int32
CAP = 12
BLOCKS = 4
CUT = 256
MSG = CAP * BLOCKS
GROUP = 4 * MSG
CHIPS = (0, 1, 7, 2, 6, 3, 5, 4)
PLACE = {k: i for i, k in enumerate(CHIPS)}
FAR_FIRST = (14, 15, 12, 13, 10, 11, 8, 9, 6, 7, 4, 5, 2, 3, 1)
ORDER = (3, 2, 1, 0)
PEERS = (10, 9, 11, 6, 14, 5, 7, 13, 15, 8, 2, 1, 3, 4, 12)
HALF = 2 * MSG
NT = (((1,), (1,)), ((), ()))
TN = (((0,), (0,)), ((), ()))


def mirror(slot):
    return 2 * PLACE[(8 - CHIPS[slot // 2]) % 8] + slot % 2


def rows(at, n):
    return pl.ds(at * n, n)


def dot(a, b, dims=(((1,), (0,)), ((), ()))):
    return lax.dot_general(a, b, dims, preferred_element_type=F32)


def kernel(
    ids_hbm, wt_hbm, tok_hbm, grad_hbm, gu_hbm, down_hbm,
    mixed_ref, tgrad_ref, rwg_ref, wgrad_ref,
    ids_ref, wt_ref, tok, grad, gu, down, spread, gather, perm, picks,
    snd_t, snd_g, rcv_t, rcv_g, xs, gs, p1, p2, e_snd, e_all, l_snd, l_all,
    out_r, out_d, ret_r, ret_d, part, own, got,
    ld_sem, t_ss, t_rs, g_ss, g_rs, r_ss, r_rs, d_ss, d_rs,
    e_ss, e_rs, l_ss, l_rs, w_ss, w_rs,
):
    dp, ex = lax.axis_index("dp"), lax.axis_index("expert")
    y, z = lax.rem(dp, 8), lax.div(dp, 8)
    x, core = lax.div(ex, 2), lax.rem(ex, 2)

    def expert_at(slot):
        chip = lax.rem(x + CHIPS[slot // 2], 8)
        return {"expert": chip * 2 + (core if slot % 2 == 0 else 1 - core)}

    def dp_at(yy, zz):
        return {"dp": zz * 8 + yy}

    y0, z0 = y + 1 - 2 * lax.rem(y, 2), z + 1 - 2 * lax.rem(z, 2)
    y1, z1 = lax.rem(y + 7 + 2 * lax.rem(y, 2), 8), lax.rem(z + 7 + 2 * lax.rem(z, 2), 8)
    quads = (
        (dp_at(y0, z), dp_at(y, z0), dp_at(y0, z0)),
        (dp_at(y1, z), dp_at(y, z1), dp_at(y1, z1)),
    )

    def peer(m):
        return lax.rem(y + 2 * (m % 4), 8), lax.rem(z + 2 * (m // 4), 8)

    loads = [
        pltpu.make_async_copy(ids_hbm, ids_ref, ld_sem.at[10]),
        pltpu.make_async_copy(wt_hbm, wt_ref, ld_sem.at[11]),
    ]
    for b in range(BLOCKS):
        loads.append(pltpu.make_async_copy(tok_hbm.at[:, rows(b, CUT)], tok.at[rows(b, 128)], ld_sem.at[b]))
    for b in range(BLOCKS):
        loads.append(pltpu.make_async_copy(grad_hbm.at[:, rows(b, CUT)], grad.at[rows(b, 128)], ld_sem.at[4 + b]))
    loads.append(pltpu.make_async_copy(gu_hbm.at[0], gu, ld_sem.at[8]))
    loads.append(pltpu.make_async_copy(down_hbm.at[0], down, ld_sem.at[9]))

    barrier = pltpu.get_barrier_semaphore()
    for load in loads[:2]:
        load.start()
    for slot in FAR_FIRST:
        pl.semaphore_signal(barrier, 1, device_id=expert_at(slot), device_id_type=MESH)
    for load in loads[2:]:
        load.start()
    for m in PEERS:
        pl.semaphore_signal(barrier, 1, device_id=dp_at(*peer(m)), device_id_type=MESH)
    for quad in quads:
        for device in quad:
            pl.semaphore_signal(barrier, 1, device_id=device, device_id_type=MESH)

    sub = lax.broadcasted_iota(I32, (128, 128), 0)
    lane = lax.broadcasted_iota(I32, (128, 128), 1)
    eye = sub == lane

    def column(row):
        return jnp.sum(jnp.where(eye, row, 0.0), axis=1, keepdims=True)

    loads[0].wait()
    loads[1].wait()
    ids = ids_ref[...]
    chip = ((ids >> 1) + (8 - x)) & 7
    place = jnp.where(chip > 4, 16 - 2 * chip, jnp.where(chip == 0, 0, 2 * chip - 1))
    slot_row = (2 * place + ((ids + core) & 1)).astype(F32)
    slot_col = column(slot_row)
    same = slot_row == slot_col
    before_row = jnp.sum(jnp.where(same & (sub < lane), 1.0, 0.0), axis=0, keepdims=True)
    before_col = jnp.sum(jnp.where(same & (lane < sub), 1.0, 0.0), axis=1, keepdims=True)
    at_row = (slot_row * float(MSG) + before_row).astype(I32)
    at_col = (slot_col * float(MSG) + before_col).astype(I32)
    weight = column(wt_ref[...])

    down_rows = lax.broadcasted_iota(I32, (16 * MSG, 128), 0)
    for b in range(BLOCKS):
        spread[:, b * 128:(b + 1) * 128] = jnp.where(down_rows == at_row + CAP * b, 1.0, 0.0).astype(BF16)
    for b in range(BLOCKS):
        loads[2 + b].wait()
    snd_t[...] = dot(spread[...], tok[...]).astype(BF16)

    pl.semaphore_wait(barrier, 36)

    def exchange(slot, src, dst, ss, rs):
        other = mirror(slot)
        return pltpu.make_async_remote_copy(
            src.at[rows(slot, MSG)], dst.at[rows(other, MSG)], ss.at[slot], rs.at[other],
            device_id=expert_at(slot), device_id_type=MESH,
        )

    def arrival(slot, src, dst, ss, rs):
        return pltpu.make_async_remote_copy(
            src.at[rows(slot, MSG)], dst.at[rows(slot, MSG)], ss.at[slot], rs.at[slot],
            device_id=expert_at(slot), device_id_type=MESH,
        )

    tset, gset = (snd_t, rcv_t, t_ss, t_rs), (snd_g, rcv_g, g_ss, g_rs)
    rset, dset = (out_r, ret_r, r_ss, r_rs), (out_d, ret_d, d_ss, d_rs)
    for slot in FAR_FIRST:
        exchange(slot, *tset).start()
    for b in range(BLOCKS):
        loads[6 + b].wait()
    for b in range(BLOCKS):
        grad_b = grad[rows(b, 128), :].astype(F32)
        tok[rows(b, 128), :] = (weight * grad_b).astype(BF16)
    snd_g[...] = dot(spread[...], tok[...]).astype(BF16)
    for slot in FAR_FIRST:
        exchange(slot, *gset).start()
    rcv_t[0:MSG, :] = snd_t[0:MSG, :]
    rcv_g[0:MSG, :] = snd_g[0:MSG, :]

    up = lax.broadcasted_iota(I32, (GROUP, GROUP), 0)
    across = lax.broadcasted_iota(I32, (GROUP, GROUP), 1)
    twelfth = (up * 5462) >> 16
    target = (twelfth & 3) * MSG + (twelfth >> 2) * CAP + (up - twelfth * CAP)
    perm[...] = jnp.where(across == target, 1.0, 0.0).astype(BF16)
    for b in range(BLOCKS):
        right = lax.broadcasted_iota(I32, (128, 16 * MSG), 1)
        gather[rows(b, 128), :] = jnp.where(right == at_col + CAP * b, 1.0, 0.0).astype(BF16)

    lanes_in = lax.broadcasted_iota(I32, (256, 128), 0)
    lanes_out = lax.broadcasted_iota(I32, (256, 128), 1)
    goal = (lanes_in >> 7) * 64 + ((lanes_in >> 5) & 3) * 16 + (lanes_in & 15)
    odd_y, odd_z = lax.rem(y, 2), lax.rem(z, 2)
    for flip in range(2):
        parity = odd_y if flip == 0 else 1 - odd_y
        picks[flip] = jnp.where((lanes_out == goal) & (((lanes_in >> 4) & 1) == parity), 1.0, 0.0).astype(BF16)

    def pack(buf, at):
        classes = [None] * 4
        for flip in range(2):
            pieces = []
            for odd in (odd_z, 1 - odd_z):
                for h in range(2):
                    left = pl.ds(pl.multiple_of((odd + 4 * h) * 128, 128), 128)
                    right = pl.ds(pl.multiple_of((odd + 4 * h + 2) * 128, 128), 128)
                    pieces.append(jnp.concatenate([buf[at, left], buf[at, right]], axis=1))
            chosen = dot(jnp.concatenate(pieces, axis=0), picks[flip]).astype(BF16)
            for k in range(2):
                classes[flip + 2 * k] = (
                    chosen[2 * k * HALF:(2 * k + 1) * HALF, :], chosen[(2 * k + 1) * HALF:(2 * k + 2) * HALF, :]
                )
        return classes

    def forward(group, m, src, dst, ss, rs):
        return pltpu.make_async_remote_copy(
            src.at[rows(4 * (m - 1) + group, MSG)], dst.at[rows(4 * m + group, MSG)],
            ss.at[4 * m + group], rs.at[4 * m + group],
            device_id=quads[group % 2][m - 1], device_id_type=MESH,
        )

    eset, lset = (e_snd, e_all, e_ss, e_rs), (l_snd, l_all, l_ss, l_rs)

    def take(group, kind, buf):
        for slot in range(4 * group + 3, 4 * group - 1, -1):
            if slot:
                arrival(slot, *kind).wait_recv()
        turned = dot(perm[...], kind[1][rows(group, GROUP), :]).astype(BF16)
        for b in range(BLOCKS):
            buf[rows(group, MSG), b * CUT:(b + 1) * CUT] = turned[b * MSG:(b + 1) * MSG, :]

    def spill(half, classes, width, values, kind):
        at = rows(half, HALF)
        for m in (3, 2, 1, 0):
            buf = kind[0] if m else kind[1]
            place = pl.ds((GROUP * (m - 1) if m else 0) + half * HALF, HALF)
            buf[place, 0:128] = classes[m][0]
            buf[place, 128:256] = classes[m][1]
            for i, value in enumerate(values):
                buf[place, 256 + i * width:256 + (i + 1) * width] = value
            if m:
                for group in (2 * half + 1, 2 * half):
                    forward(group, m, *kind).start()

    def early(half):
        at = rows(half, HALF)
        pre = dot(xs[at, :], gu[...])
        a, u = pre[:, :384], pre[:, 384:]
        s = 1.0 / (1.0 + jnp.exp(-a))
        silu = a * s
        p1[at, :] = u * s * (1.0 + a * (1.0 - s))
        p2[at, :] = silu
        spill(half, pack(xs, at), 384, [(silu * u).astype(BF16)], eset)

    def late(half):
        at = rows(half, HALF)
        d_act = dot(gs[at, :], down[...], NT)
        spill(half, pack(gs, at), 384, [(d_act * p1[at, :]).astype(BF16), (d_act * p2[at, :]).astype(BF16)], lset)

    def give(value, kind):
        buf = kind[0]
        for group in ORDER:
            stacked = jnp.concatenate(
                [value[group * MSG:(group + 1) * MSG, b * CUT:(b + 1) * CUT] for b in range(BLOCKS)], axis=0
            )
            buf[rows(group, GROUP), :] = dot(perm[...], stacked).astype(BF16)
            for slot in range(4 * group + 3, 4 * group - 1, -1):
                if slot:
                    exchange(slot, *kind).start()

    take(3, tset, xs)
    take(2, tset, xs)
    loads[10].wait()
    loads[11].wait()
    early(1)
    take(1, tset, xs)
    take(0, tset, xs)
    early(0)
    give(dot(e_all[rows(0, GROUP), 256:640], down[...]).astype(BF16), rset)
    take(3, gset, gs)
    take(2, gset, gs)
    late(1)
    take(1, gset, gs)
    take(0, gset, gs)
    late(0)
    give(dot(l_all[rows(0, GROUP), 256:1024], gu[...], NT).astype(BF16), dset)

    def share(m):
        yy, zz = peer(m)
        other = ((4 - m // 4) % 4) * 4 + (4 - m % 4) % 4
        return pltpu.make_async_remote_copy(
            part.at[lax.div(zz, 2) * 4 + lax.div(yy, 2)], got.at[other], w_ss.at[m], w_rs.at[other],
            device_id=dp_at(yy, zz), device_id_type=MESH,
        )

    def shared(m):
        return pltpu.make_async_remote_copy(
            part.at[m], got.at[m], w_ss.at[m], w_rs.at[m],
            device_id=dp_at(*peer(m)), device_id_type=MESH,
        )

    for m in (1, 2, 3):
        for group in ORDER:
            forward(group, m, *eset).wait_recv()
            forward(group, m, *lset).wait_recv()
    first = dot(e_all[:, 0:256], l_all[:, 256:1024], TN)
    last = dot(l_all[:, 0:256], e_all[:, 256:640], TN)
    for k in range(16):
        part[k, :, 0:768] = first[k * 16:(k + 1) * 16, :].astype(BF16)
        part[k, :, 768:1152] = last[k * 16:(k + 1) * 16, :].astype(BF16)
    for m in PEERS:
        share(m).start()
    for k in range(16):
        own[k, :, 0:768] = first[k * 16:(k + 1) * 16, :]
        own[k, :, 768:1152] = last[k * 16:(k + 1) * 16, :]

    ret_r[0:MSG, :] = out_r[0:MSG, :]
    ret_d[0:MSG, :] = out_d[0:MSG, :]
    for slot in range(1, 16):
        arrival(slot, *rset).wait_recv()
    inner = jnp.zeros((128, 1), F32)
    for b in range(BLOCKS):
        copy_out = dot(gather[rows(b, 128), :], ret_r[...])
        mixed_ref[:, b * CUT:(b + 1) * CUT] = (weight * copy_out).astype(BF16)
        inner = inner + jnp.sum(grad[rows(b, 128), :].astype(F32) * copy_out, axis=1, keepdims=True)
    rwg_ref[...] = jnp.sum(jnp.where(eye, inner, 0.0), axis=0, keepdims=True)
    for slot in range(1, 16):
        arrival(slot, *dset).wait_recv()
    for b in range(BLOCKS):
        tgrad_ref[:, b * CUT:(b + 1) * CUT] = dot(gather[rows(b, 128), :], ret_d[...]).astype(BF16)

    total = own[lax.div(z, 2) * 4 + lax.div(y, 2)]
    for m in range(1, 16):
        shared(m).wait_recv()
        total = total + got[m].astype(F32)
    wgrad_ref[0] = total

    for slot in range(1, 16):
        for kind in (tset, gset, rset, dset):
            exchange(slot, *kind).wait_send()
        share(slot).wait_send()
    for group in range(4):
        for m in (1, 2, 3):
            for kind in (eset, lset):
                forward(group, m, *kind).wait_send()


def hand_over(*refs):
    taken, given, sem = refs[:4], refs[4:8], refs[8]
    copies = [pltpu.make_async_copy(a, b, sem.at[i]) for i, (a, b) in enumerate(zip(taken, given))]
    for copy in copies:
        copy.start()
    for copy in copies:
        copy.wait()


def on_device(tokens, route_ids, route_weight, w_gate_up, w_down, out_grad):
    count, width = tokens.shape
    hidden = w_down.shape[1]
    dma = pltpu.SemaphoreType.DMA
    vmem = pl.BlockSpec(memory_space=pltpu.VMEM)
    hbm = pl.BlockSpec(memory_space=pl.ANY)
    slots = 16 * MSG
    scratch = [
        pltpu.VMEM((1, count), I32), pltpu.VMEM((1, count), F32),
        pltpu.VMEM((512, CUT), BF16), pltpu.VMEM((512, CUT), BF16),
        pltpu.VMEM((width, 2 * hidden), BF16), pltpu.VMEM((hidden, width), BF16),
        pltpu.VMEM((slots, 512), BF16), pltpu.VMEM((512, slots), BF16), pltpu.VMEM((GROUP, GROUP), BF16),
        pltpu.VMEM((2, 256, 128), BF16),
        *[pltpu.VMEM((slots, CUT), BF16)] * 4,
        pltpu.VMEM((GROUP, width), BF16), pltpu.VMEM((GROUP, width), BF16),
        pltpu.VMEM((GROUP, hidden), F32), pltpu.VMEM((GROUP, hidden), F32),
        pltpu.VMEM((3 * GROUP, 256 + hidden), BF16), pltpu.VMEM((4 * GROUP, 256 + hidden), BF16),
        pltpu.VMEM((3 * GROUP, 256 + 2 * hidden), BF16), pltpu.VMEM((4 * GROUP, 256 + 2 * hidden), BF16),
        *[pltpu.VMEM((slots, CUT), BF16)] * 4,
        pltpu.VMEM((16, 16, 3 * hidden), BF16), pltpu.VMEM((16, 16, 3 * hidden), F32),
        pltpu.VMEM((16, 16, 3 * hidden), BF16),
        dma((12,)), *[dma((16,))] * 14,
    ]
    outs = (
        jax.ShapeDtypeStruct((count, width), BF16),
        jax.ShapeDtypeStruct((count, width), BF16),
        jax.ShapeDtypeStruct((1, count), F32),
        jax.ShapeDtypeStruct((1, 16, 3 * hidden), F32),
    )
    made = pl.pallas_call(
        kernel,
        out_shape=outs,
        in_specs=[hbm] * 6,
        out_specs=[vmem] * 4,
        scratch_shapes=scratch,
        compiler_params=pltpu.CompilerParams(
            collective_id=0, has_side_effects=True, vmem_limit_bytes=58 * 2**20
        ),
    )(route_ids.reshape(1, count), route_weight.reshape(1, count), tokens, out_grad, w_gate_up, w_down)
    mixed, tgrad, rwg, wgrad = pl.pallas_call(
        hand_over,
        out_shape=outs,
        in_specs=[vmem] * 4,
        out_specs=[hbm] * 4,
        scratch_shapes=[dma((4,))],
    )(*made)
    return mixed, tgrad, rwg.reshape(count, 1), wgrad


def solution(mesh):
    rows_split = P(("dp", "expert"), None)
    return jax.shard_map(
        on_device,
        mesh=mesh,
        in_specs=(rows_split, rows_split, rows_split, P("expert", None, None), P("expert", None, None), rows_split),
        out_specs=(rows_split, rows_split, rows_split, P("expert", "dp", None)),
        check_vma=False,
    )
```

```python
import jax
import jax.numpy as jnp
from jax import lax
from jax.experimental import pallas as pl
from jax.experimental.pallas import tpu as pltpu
from jax.sharding import PartitionSpec as P

MESH = pl.DeviceIdType.MESH
BF16, F32, I32 = jnp.bfloat16, jnp.float32, jnp.int32
CAP = 12
BLOCKS = 4
CUT = 256
MSG = CAP * BLOCKS
GROUP = 4 * MSG
CHIPS = (0, 1, 7, 2, 6, 3, 5, 4)
PLACE = {k: i for i, k in enumerate(CHIPS)}
FAR_FIRST = (14, 15, 12, 13, 10, 11, 8, 9, 6, 7, 4, 5, 2, 3, 1)
ORDER = (3, 2, 1, 0)
PEERS = (10, 9, 11, 6, 14, 5, 7, 13, 15, 8, 2, 1, 3, 4, 12)
HALF = 2 * MSG
NT = (((1,), (1,)), ((), ()))
TN = (((0,), (0,)), ((), ()))


def mirror(slot):
    return 2 * PLACE[(8 - CHIPS[slot // 2]) % 8] + slot % 2


def rows(at, n):
    return pl.ds(at * n, n)


def dot(a, b, dims=(((1,), (0,)), ((), ()))):
    return lax.dot_general(a, b, dims, preferred_element_type=F32)


def kernel(
    ids_hbm, wt_hbm, tok_hbm, grad_hbm, gu_hbm, down_hbm,
    mixed_ref, tgrad_ref, rwg_ref, wgrad_ref,
    ids_ref, wt_ref, tok, grad, gu, down, spread, gather, perm, picks,
    snd_t, snd_g, rcv_t, rcv_g, xs, gs, p1, p2, e_snd, e_all, l_snd, l_all,
    out_r, out_d, ret_r, ret_d, part, own, got,
    ld_sem, t_ss, t_rs, g_ss, g_rs, r_ss, r_rs, d_ss, d_rs,
    e_ss, e_rs, l_ss, l_rs, w_ss, w_rs, here,
):
    dp, ex = lax.axis_index("dp"), lax.axis_index("expert")
    y, z = lax.rem(dp, 8), lax.div(dp, 8)
    x, core = lax.div(ex, 2), lax.rem(ex, 2)

    def expert_at(slot):
        chip = lax.rem(x + CHIPS[slot // 2], 8)
        return {"expert": chip * 2 + (core if slot % 2 == 0 else 1 - core)}

    def dp_at(yy, zz):
        return {"dp": zz * 8 + yy}

    y0, z0 = y + 1 - 2 * lax.rem(y, 2), z + 1 - 2 * lax.rem(z, 2)
    y1, z1 = lax.rem(y + 7 + 2 * lax.rem(y, 2), 8), lax.rem(z + 7 + 2 * lax.rem(z, 2), 8)
    quads = (
        (dp_at(y0, z), dp_at(y, z0), dp_at(y0, z0)),
        (dp_at(y1, z), dp_at(y, z1), dp_at(y1, z1)),
    )

    def peer(m):
        return lax.rem(y + 2 * (m % 4), 8), lax.rem(z + 2 * (m // 4), 8)

    loads = [
        pltpu.make_async_copy(ids_hbm, ids_ref, ld_sem.at[10]),
        pltpu.make_async_copy(wt_hbm, wt_ref, ld_sem.at[11]),
    ]
    for b in range(BLOCKS):
        loads.append(pltpu.make_async_copy(tok_hbm.at[:, rows(b, CUT)], tok.at[rows(b, 128)], ld_sem.at[b]))
    for b in range(BLOCKS):
        loads.append(pltpu.make_async_copy(grad_hbm.at[:, rows(b, CUT)], grad.at[rows(b, 128)], ld_sem.at[4 + b]))
    loads.append(pltpu.make_async_copy(gu_hbm.at[0], gu, ld_sem.at[8]))
    loads.append(pltpu.make_async_copy(down_hbm.at[0], down, ld_sem.at[9]))

    barrier = pltpu.get_barrier_semaphore()
    for load in loads[:2]:
        load.start()
    for slot in FAR_FIRST:
        pl.semaphore_signal(barrier, 1, device_id=expert_at(slot), device_id_type=MESH)
    for m in (2, 1, 3):
        pl.semaphore_signal(barrier, 1, device_id=dp_at(*peer(m)), device_id_type=MESH)
    for quad in quads:
        for device in quad:
            pl.semaphore_signal(barrier, 1, device_id=device, device_id_type=MESH)
    for load in loads[2:]:
        load.start()

    sub = lax.broadcasted_iota(I32, (128, 128), 0)
    lane = lax.broadcasted_iota(I32, (128, 128), 1)
    eye = sub == lane

    def column(row):
        return jnp.sum(jnp.where(eye, row, 0.0), axis=1, keepdims=True)

    loads[0].wait()
    loads[1].wait()
    ids = ids_ref[...]
    chip = ((ids >> 1) + (8 - x)) & 7
    place = jnp.where(chip > 4, 16 - 2 * chip, jnp.where(chip == 0, 0, 2 * chip - 1))
    slot_row = (2 * place + ((ids + core) & 1)).astype(F32)
    slot_col = column(slot_row)
    same = slot_row == slot_col
    before_row = jnp.sum(jnp.where(same & (sub < lane), 1.0, 0.0), axis=0, keepdims=True)
    before_col = jnp.sum(jnp.where(same & (lane < sub), 1.0, 0.0), axis=1, keepdims=True)
    at_row = (slot_row * float(MSG) + before_row).astype(I32)
    at_col = (slot_col * float(MSG) + before_col).astype(I32)
    weight = column(wt_ref[...])

    down_rows = lax.broadcasted_iota(I32, (16 * MSG, 128), 0)
    for b in range(BLOCKS):
        spread[:, b * 128:(b + 1) * 128] = jnp.where(down_rows == at_row + CAP * b, 1.0, 0.0).astype(BF16)
    for b in range(BLOCKS):
        loads[2 + b].wait()
    snd_t[...] = dot(spread[...], tok[...]).astype(BF16)

    pl.semaphore_wait(barrier, 24)

    def exchange(slot, src, dst, ss, rs):
        other = mirror(slot)
        return pltpu.make_async_remote_copy(
            src.at[rows(slot, MSG)], dst.at[rows(other, MSG)], ss.at[slot], rs.at[other],
            device_id=expert_at(slot), device_id_type=MESH,
        )

    def arrival(slot, src, dst, ss, rs):
        return pltpu.make_async_remote_copy(
            src.at[rows(slot, MSG)], dst.at[rows(slot, MSG)], ss.at[slot], rs.at[slot],
            device_id=expert_at(slot), device_id_type=MESH,
        )

    tset, gset = (snd_t, rcv_t, t_ss, t_rs), (snd_g, rcv_g, g_ss, g_rs)
    rset, dset = (out_r, ret_r, r_ss, r_rs), (out_d, ret_d, d_ss, d_rs)
    for slot in FAR_FIRST:
        exchange(slot, *tset).start()
    for b in range(BLOCKS):
        loads[6 + b].wait()
    for b in range(BLOCKS):
        grad_b = grad[rows(b, 128), :].astype(F32)
        tok[rows(b, 128), :] = (weight * grad_b).astype(BF16)
    snd_g[...] = dot(spread[...], tok[...]).astype(BF16)
    for slot in FAR_FIRST:
        exchange(slot, *gset).start()

    def tell(i, zz):
        pl.semaphore_signal(here.at[i], 1, device_id=dp_at(y, zz), device_id_type=MESH)

    tell(0, z0)
    tell(1, z1)
    rcv_t[0:MSG, :] = snd_t[0:MSG, :]
    rcv_g[0:MSG, :] = snd_g[0:MSG, :]

    up = lax.broadcasted_iota(I32, (GROUP, GROUP), 0)
    across = lax.broadcasted_iota(I32, (GROUP, GROUP), 1)
    twelfth = (up * 5462) >> 16
    target = (twelfth & 3) * MSG + (twelfth >> 2) * CAP + (up - twelfth * CAP)
    perm[...] = jnp.where(across == target, 1.0, 0.0).astype(BF16)
    for b in range(BLOCKS):
        right = lax.broadcasted_iota(I32, (128, 16 * MSG), 1)
        gather[rows(b, 128), :] = jnp.where(right == at_col + CAP * b, 1.0, 0.0).astype(BF16)

    lanes_in = lax.broadcasted_iota(I32, (256, 128), 0)
    lanes_out = lax.broadcasted_iota(I32, (256, 128), 1)
    goal = (lanes_in >> 7) * 64 + ((lanes_in >> 5) & 3) * 16 + (lanes_in & 15)
    odd_y, odd_z = lax.rem(y, 2), lax.rem(z, 2)
    for flip in range(2):
        parity = odd_y if flip == 0 else 1 - odd_y
        picks[flip] = jnp.where((lanes_out == goal) & (((lanes_in >> 4) & 1) == parity), 1.0, 0.0).astype(BF16)

    def pack(buf, at):
        classes = [None] * 4
        for flip in range(2):
            pieces = []
            for odd in (odd_z, 1 - odd_z):
                for h in range(2):
                    left = pl.ds(pl.multiple_of((odd + 4 * h) * 128, 128), 128)
                    right = pl.ds(pl.multiple_of((odd + 4 * h + 2) * 128, 128), 128)
                    pieces.append(jnp.concatenate([buf[at, left], buf[at, right]], axis=1))
            chosen = dot(jnp.concatenate(pieces, axis=0), picks[flip]).astype(BF16)
            for k in range(2):
                classes[flip + 2 * k] = (
                    chosen[2 * k * HALF:(2 * k + 1) * HALF, :], chosen[(2 * k + 1) * HALF:(2 * k + 2) * HALF, :]
                )
        return classes

    def spot(m, group):
        return (group // 2) * 8 + 2 * m + group % 2

    def forward(group, m, src, dst, ss, rs):
        return pltpu.make_async_remote_copy(
            src.at[rows(4 * (m - 1) + group, MSG)], dst.at[rows(spot(m, group), MSG)],
            ss.at[4 * m + group], rs.at[4 * m + group],
            device_id=quads[group % 2][m - 1], device_id_type=MESH,
        )

    eset, lset = (e_snd, e_all, e_ss, e_rs), (l_snd, l_all, l_ss, l_rs)

    def take(group, kind, buf):
        for slot in range(4 * group + 3, 4 * group - 1, -1):
            if slot:
                arrival(slot, *kind).wait_recv()
        turned = dot(perm[...], kind[1][rows(group, GROUP), :]).astype(BF16)
        for b in range(BLOCKS):
            buf[rows(group, MSG), b * CUT:(b + 1) * CUT] = turned[b * MSG:(b + 1) * MSG, :]

    def spill(half, classes, width, values, kind):
        for m in (3, 2, 1, 0):
            buf = kind[0] if m else kind[1]
            place = pl.ds(GROUP * (m - 1) + half * HALF if m else 4 * half * HALF, HALF)
            buf[place, 0:128] = classes[m][0]
            buf[place, 128:256] = classes[m][1]
            for i, value in enumerate(values):
                buf[place, 256 + i * width:256 + (i + 1) * width] = value
            if m:
                for group in (2 * half + 1, 2 * half):
                    forward(group, m, *kind).start()

    def early(half):
        at = rows(half, HALF)
        pre = dot(xs[at, :], gu[...])
        a, u = pre[:, :384], pre[:, 384:]
        s = 1.0 / (1.0 + jnp.exp(-a))
        silu = a * s
        p1[at, :] = u * s * (1.0 + a * (1.0 - s))
        p2[at, :] = silu
        spill(half, pack(xs, at), 384, [(silu * u).astype(BF16)], eset)

    def late(half):
        at = rows(half, HALF)
        d_act = dot(gs[at, :], down[...], NT)
        spill(half, pack(gs, at), 384, [(d_act * p1[at, :]).astype(BF16), (d_act * p2[at, :]).astype(BF16)], lset)

    def give(value, kind):
        buf = kind[0]
        for group in ORDER:
            stacked = jnp.concatenate(
                [value[group * MSG:(group + 1) * MSG, b * CUT:(b + 1) * CUT] for b in range(BLOCKS)], axis=0
            )
            buf[rows(group, GROUP), :] = dot(perm[...], stacked).astype(BF16)
            for slot in range(4 * group + 3, 4 * group - 1, -1):
                if slot:
                    exchange(slot, *kind).start()

    def mine(buf, low, high):
        return jnp.concatenate([buf[rows(4 * half, HALF), low:high] for half in range(2)], axis=0)

    take(3, tset, xs)
    take(2, tset, xs)
    loads[10].wait()
    loads[11].wait()
    early(1)
    take(1, tset, xs)
    take(0, tset, xs)
    early(0)
    give(dot(mine(e_all, 256, 640), down[...]).astype(BF16), rset)
    pl.semaphore_wait(here.at[0], 1)
    pl.semaphore_wait(here.at[1], 1)
    tell(2, lax.rem(z + 2, 8))
    tell(3, lax.rem(z + 6, 8))
    take(3, gset, gs)
    take(2, gset, gs)
    late(1)
    pl.semaphore_wait(here.at[2], 1)
    pl.semaphore_wait(here.at[3], 1)
    tell(4, lax.rem(z + 4, 8))
    take(1, gset, gs)
    take(0, gset, gs)
    late(0)
    give(dot(mine(l_all, 256, 1024), gu[...], NT).astype(BF16), dset)

    def share(m):
        yy, zz = peer(m)
        other = ((4 - m // 4) % 4) * 4 + (4 - m % 4) % 4
        return pltpu.make_async_remote_copy(
            part.at[lax.div(zz, 2) * 4 + lax.div(yy, 2)], got.at[other], w_ss.at[m], w_rs.at[other],
            device_id=dp_at(yy, zz), device_id_type=MESH,
        )

    def shared(m):
        return pltpu.make_async_remote_copy(
            part.at[m], got.at[m], w_ss.at[m], w_rs.at[m],
            device_id=dp_at(*peer(m)), device_id_type=MESH,
        )

    first = last = 0.0
    for half in (1, 0):
        for m in (1, 2, 3):
            for group in (2 * half + 1, 2 * half):
                forward(group, m, *eset).wait_recv()
                forward(group, m, *lset).wait_recv()
        at = rows(half, 4 * HALF)
        first = first + dot(e_all[at, 0:256], l_all[at, 256:1024], TN)
        last = last + dot(l_all[at, 0:256], e_all[at, 256:640], TN)
    pl.semaphore_wait(here.at[4], 1)
    for k in range(16):
        part[k, :, 0:768] = first[k * 16:(k + 1) * 16, :].astype(BF16)
        part[k, :, 768:1152] = last[k * 16:(k + 1) * 16, :].astype(BF16)
    for m in PEERS:
        share(m).start()
    for k in range(16):
        own[k, :, 0:768] = first[k * 16:(k + 1) * 16, :]
        own[k, :, 768:1152] = last[k * 16:(k + 1) * 16, :]

    ret_r[0:MSG, :] = out_r[0:MSG, :]
    ret_d[0:MSG, :] = out_d[0:MSG, :]
    for slot in range(1, 16):
        arrival(slot, *rset).wait_recv()
    inner = jnp.zeros((128, 1), F32)
    for b in range(BLOCKS):
        copy_out = dot(gather[rows(b, 128), :], ret_r[...])
        mixed_ref[:, b * CUT:(b + 1) * CUT] = (weight * copy_out).astype(BF16)
        inner = inner + jnp.sum(grad[rows(b, 128), :].astype(F32) * copy_out, axis=1, keepdims=True)
    rwg_ref[...] = jnp.sum(jnp.where(eye, inner, 0.0), axis=0, keepdims=True)
    for slot in range(1, 16):
        arrival(slot, *dset).wait_recv()
    for b in range(BLOCKS):
        tgrad_ref[:, b * CUT:(b + 1) * CUT] = dot(gather[rows(b, 128), :], ret_d[...]).astype(BF16)

    total = own[lax.div(z, 2) * 4 + lax.div(y, 2)]
    for m in range(1, 16):
        shared(m).wait_recv()
        total = total + got[m].astype(F32)
    wgrad_ref[0] = total

    for slot in range(1, 16):
        for kind in (tset, gset, rset, dset):
            exchange(slot, *kind).wait_send()
        share(slot).wait_send()
    for group in range(4):
        for m in (1, 2, 3):
            for kind in (eset, lset):
                forward(group, m, *kind).wait_send()


def hand_over(*refs):
    taken, given, sem = refs[:4], refs[4:8], refs[8]
    copies = [pltpu.make_async_copy(a, b, sem.at[i]) for i, (a, b) in enumerate(zip(taken, given))]
    for copy in copies:
        copy.start()
    for copy in copies:
        copy.wait()


def on_device(tokens, route_ids, route_weight, w_gate_up, w_down, out_grad):
    count, width = tokens.shape
    hidden = w_down.shape[1]
    dma = pltpu.SemaphoreType.DMA
    vmem = pl.BlockSpec(memory_space=pltpu.VMEM)
    hbm = pl.BlockSpec(memory_space=pl.ANY)
    slots = 16 * MSG
    scratch = [
        pltpu.VMEM((1, count), I32), pltpu.VMEM((1, count), F32),
        pltpu.VMEM((512, CUT), BF16), pltpu.VMEM((512, CUT), BF16),
        pltpu.VMEM((width, 2 * hidden), BF16), pltpu.VMEM((hidden, width), BF16),
        pltpu.VMEM((slots, 512), BF16), pltpu.VMEM((512, slots), BF16), pltpu.VMEM((GROUP, GROUP), BF16),
        pltpu.VMEM((2, 256, 128), BF16),
        *[pltpu.VMEM((slots, CUT), BF16)] * 4,
        pltpu.VMEM((GROUP, width), BF16), pltpu.VMEM((GROUP, width), BF16),
        pltpu.VMEM((GROUP, hidden), F32), pltpu.VMEM((GROUP, hidden), F32),
        pltpu.VMEM((3 * GROUP, 256 + hidden), BF16), pltpu.VMEM((4 * GROUP, 256 + hidden), BF16),
        pltpu.VMEM((3 * GROUP, 256 + 2 * hidden), BF16), pltpu.VMEM((4 * GROUP, 256 + 2 * hidden), BF16),
        *[pltpu.VMEM((slots, CUT), BF16)] * 4,
        pltpu.VMEM((16, 16, 3 * hidden), BF16), pltpu.VMEM((16, 16, 3 * hidden), F32),
        pltpu.VMEM((16, 16, 3 * hidden), BF16),
        dma((12,)), *[dma((16,))] * 14,
        pltpu.SemaphoreType.REGULAR((5,)),
    ]
    outs = (
        jax.ShapeDtypeStruct((count, width), BF16),
        jax.ShapeDtypeStruct((count, width), BF16),
        jax.ShapeDtypeStruct((1, count), F32),
        jax.ShapeDtypeStruct((1, 16, 3 * hidden), F32),
    )
    made = pl.pallas_call(
        kernel,
        out_shape=tuple(pltpu.VMEM(o.shape, o.dtype) for o in outs),
        in_specs=[hbm] * 6,
        out_specs=[vmem] * 4,
        scratch_shapes=scratch,
        compiler_params=pltpu.CompilerParams(
            collective_id=0, has_side_effects=True, vmem_limit_bytes=58 * 2**20
        ),
    )(route_ids.reshape(1, count), route_weight.reshape(1, count), tokens, out_grad, w_gate_up, w_down)
    mixed, tgrad, rwg, wgrad = pl.pallas_call(
        hand_over,
        out_shape=outs,
        in_specs=[vmem] * 4,
        out_specs=[hbm] * 4,
        scratch_shapes=[dma((4,))],
        compiler_params=pltpu.CompilerParams(vmem_limit_bytes=2**21),
    )(*made)
    return mixed, tgrad, rwg.reshape(count, 1), wgrad


def solution(mesh):
    rows_split = P(("dp", "expert"), None)
    return jax.shard_map(
        on_device,
        mesh=mesh,
        in_specs=(rows_split, rows_split, rows_split, P("expert", None, None), P("expert", None, None), rows_split),
        out_specs=(rows_split, rows_split, rows_split, P("expert", "dp", None)),
        check_vma=False,
    )
```

```python
import jax
import jax.numpy as jnp
from jax import lax
from jax.experimental import pallas as pl
from jax.experimental.pallas import tpu as pltpu
from jax.sharding import PartitionSpec as P

MESH = pl.DeviceIdType.MESH
BF16, F32, I32 = jnp.bfloat16, jnp.float32, jnp.int32
CAP = 12
BLOCKS = 4
CUT = 256
MSG = CAP * BLOCKS
GROUP = 4 * MSG
CHIPS = (0, 1, 7, 2, 6, 3, 5, 4)
PLACE = {k: i for i, k in enumerate(CHIPS)}
FAR_FIRST = (14, 15, 12, 13, 10, 11, 8, 9, 6, 7, 4, 5, 2, 3, 1)
ORDER = (3, 2, 1, 0)
PEERS = (10, 9, 11, 6, 14, 5, 7, 13, 15, 8, 2, 1, 3, 4, 12)
HALF = 2 * MSG
NT = (((1,), (1,)), ((), ()))
TN = (((0,), (0,)), ((), ()))


def mirror(slot):
    return 2 * PLACE[(8 - CHIPS[slot // 2]) % 8] + slot % 2


def rows(at, n):
    return pl.ds(at * n, n)


def dot(a, b, dims=(((1,), (0,)), ((), ()))):
    return lax.dot_general(a, b, dims, preferred_element_type=F32)


def kernel(
    ids_hbm, wt_hbm, tok_hbm, grad_hbm, gu_hbm, down_hbm,
    mixed_ref, tgrad_ref, rwg_ref, wgrad_ref,
    ids_ref, wt_ref, tok, grad, gu, down, spread, gather, perm, picks,
    snd_t, snd_g, rcv_t, rcv_g, xs, gs, p1, p2, e_snd, e_all, c_snd, c_all, l_snd, l_all,
    out_r, out_d, ret_r, ret_d, part, own, got, part_c, own_c, got_c,
    ld_sem, t_ss, t_rs, g_ss, g_rs, r_ss, r_rs, d_ss, d_rs,
    e_ss, e_rs, l_ss, l_rs, w_ss, w_rs, c_ss, c_rs, v_ss, v_rs, here,
):
    dp, ex = lax.axis_index("dp"), lax.axis_index("expert")
    y, z = lax.rem(dp, 8), lax.div(dp, 8)
    x, core = lax.div(ex, 2), lax.rem(ex, 2)

    def expert_at(slot):
        chip = lax.rem(x + CHIPS[slot // 2], 8)
        return {"expert": chip * 2 + (core if slot % 2 == 0 else 1 - core)}

    def dp_at(yy, zz):
        return {"dp": zz * 8 + yy}

    y0, z0 = y + 1 - 2 * lax.rem(y, 2), z + 1 - 2 * lax.rem(z, 2)
    y1, z1 = lax.rem(y + 7 + 2 * lax.rem(y, 2), 8), lax.rem(z + 7 + 2 * lax.rem(z, 2), 8)
    quads = (
        (dp_at(y0, z), dp_at(y, z0), dp_at(y0, z0)),
        (dp_at(y1, z), dp_at(y, z1), dp_at(y1, z1)),
    )

    def peer(m):
        return lax.rem(y + 2 * (m % 4), 8), lax.rem(z + 2 * (m // 4), 8)

    loads = [
        pltpu.make_async_copy(ids_hbm, ids_ref, ld_sem.at[10]),
        pltpu.make_async_copy(wt_hbm, wt_ref, ld_sem.at[11]),
    ]
    for b in range(BLOCKS):
        loads.append(pltpu.make_async_copy(tok_hbm.at[:, rows(b, CUT)], tok.at[rows(b, 128)], ld_sem.at[b]))
    for b in range(BLOCKS):
        loads.append(pltpu.make_async_copy(grad_hbm.at[:, rows(b, CUT)], grad.at[rows(b, 128)], ld_sem.at[4 + b]))
    loads.append(pltpu.make_async_copy(gu_hbm.at[0], gu, ld_sem.at[8]))
    loads.append(pltpu.make_async_copy(down_hbm.at[0], down, ld_sem.at[9]))

    barrier = pltpu.get_barrier_semaphore()
    for load in loads[:2]:
        load.start()
    for slot in FAR_FIRST:
        pl.semaphore_signal(barrier, 1, device_id=expert_at(slot), device_id_type=MESH)
    for m in (2, 1, 3):
        pl.semaphore_signal(barrier, 1, device_id=dp_at(*peer(m)), device_id_type=MESH)
    for quad in quads:
        for device in quad:
            pl.semaphore_signal(barrier, 1, device_id=device, device_id_type=MESH)
    for load in loads[2:]:
        load.start()

    sub = lax.broadcasted_iota(I32, (128, 128), 0)
    lane = lax.broadcasted_iota(I32, (128, 128), 1)
    eye = sub == lane

    def column(row):
        return jnp.sum(jnp.where(eye, row, 0.0), axis=1, keepdims=True)

    loads[0].wait()
    loads[1].wait()
    ids = ids_ref[...]
    chip = ((ids >> 1) + (8 - x)) & 7
    place = jnp.where(chip > 4, 16 - 2 * chip, jnp.where(chip == 0, 0, 2 * chip - 1))
    slot_row = (2 * place + ((ids + core) & 1)).astype(F32)
    slot_col = column(slot_row)
    same = slot_row == slot_col
    before_row = jnp.sum(jnp.where(same & (sub < lane), 1.0, 0.0), axis=0, keepdims=True)
    before_col = jnp.sum(jnp.where(same & (lane < sub), 1.0, 0.0), axis=1, keepdims=True)
    at_row = (slot_row * float(MSG) + before_row).astype(I32)
    at_col = (slot_col * float(MSG) + before_col).astype(I32)
    weight = column(wt_ref[...])

    down_rows = lax.broadcasted_iota(I32, (16 * MSG, 128), 0)
    for b in range(BLOCKS):
        spread[:, b * 128:(b + 1) * 128] = jnp.where(down_rows == at_row + CAP * b, 1.0, 0.0).astype(BF16)
    for b in range(BLOCKS):
        loads[2 + b].wait()
    snd_t[...] = dot(spread[...], tok[...]).astype(BF16)

    pl.semaphore_wait(barrier, 24)

    def exchange(slot, src, dst, ss, rs):
        other = mirror(slot)
        return pltpu.make_async_remote_copy(
            src.at[rows(slot, MSG)], dst.at[rows(other, MSG)], ss.at[slot], rs.at[other],
            device_id=expert_at(slot), device_id_type=MESH,
        )

    def arrival(slot, src, dst, ss, rs):
        return pltpu.make_async_remote_copy(
            src.at[rows(slot, MSG)], dst.at[rows(slot, MSG)], ss.at[slot], rs.at[slot],
            device_id=expert_at(slot), device_id_type=MESH,
        )

    tset, gset = (snd_t, rcv_t, t_ss, t_rs), (snd_g, rcv_g, g_ss, g_rs)
    rset, dset = (out_r, ret_r, r_ss, r_rs), (out_d, ret_d, d_ss, d_rs)
    for slot in FAR_FIRST:
        exchange(slot, *tset).start()
    for b in range(BLOCKS):
        loads[6 + b].wait()
    for b in range(BLOCKS):
        grad_b = grad[rows(b, 128), :].astype(F32)
        tok[rows(b, 128), :] = (weight * grad_b).astype(BF16)
    snd_g[...] = dot(spread[...], tok[...]).astype(BF16)
    for slot in FAR_FIRST:
        exchange(slot, *gset).start()

    def tell(i, zz):
        pl.semaphore_signal(here.at[i], 1, device_id=dp_at(y, zz), device_id_type=MESH)

    tell(0, z0)
    tell(1, z1)
    rcv_t[0:MSG, :] = snd_t[0:MSG, :]
    rcv_g[0:MSG, :] = snd_g[0:MSG, :]

    up = lax.broadcasted_iota(I32, (GROUP, GROUP), 0)
    across = lax.broadcasted_iota(I32, (GROUP, GROUP), 1)
    twelfth = (up * 5462) >> 16
    target = (twelfth & 3) * MSG + (twelfth >> 2) * CAP + (up - twelfth * CAP)
    perm[...] = jnp.where(across == target, 1.0, 0.0).astype(BF16)
    for b in range(BLOCKS):
        right = lax.broadcasted_iota(I32, (128, 16 * MSG), 1)
        gather[rows(b, 128), :] = jnp.where(right == at_col + CAP * b, 1.0, 0.0).astype(BF16)

    lanes_in = lax.broadcasted_iota(I32, (256, 128), 0)
    lanes_out = lax.broadcasted_iota(I32, (256, 128), 1)
    goal = (lanes_in >> 7) * 64 + ((lanes_in >> 5) & 3) * 16 + (lanes_in & 15)
    odd_y, odd_z = lax.rem(y, 2), lax.rem(z, 2)
    for flip in range(2):
        parity = odd_y if flip == 0 else 1 - odd_y
        picks[flip] = jnp.where((lanes_out == goal) & (((lanes_in >> 4) & 1) == parity), 1.0, 0.0).astype(BF16)

    def pack(buf, at):
        classes = [None] * 4
        for flip in range(2):
            pieces = []
            for odd in (odd_z, 1 - odd_z):
                for h in range(2):
                    left = pl.ds(pl.multiple_of((odd + 4 * h) * 128, 128), 128)
                    right = pl.ds(pl.multiple_of((odd + 4 * h + 2) * 128, 128), 128)
                    pieces.append(jnp.concatenate([buf[at, left], buf[at, right]], axis=1))
            chosen = dot(jnp.concatenate(pieces, axis=0), picks[flip]).astype(BF16)
            for k in range(2):
                classes[flip + 2 * k] = (
                    chosen[2 * k * HALF:(2 * k + 1) * HALF, :], chosen[(2 * k + 1) * HALF:(2 * k + 2) * HALF, :]
                )
        return classes

    def spot(m, group):
        return (group // 2) * 8 + 2 * m + group % 2

    def forward(group, m, src, dst, ss, rs):
        return pltpu.make_async_remote_copy(
            src.at[rows(4 * (m - 1) + group, MSG)], dst.at[rows(spot(m, group), MSG)],
            ss.at[4 * m + group], rs.at[4 * m + group],
            device_id=quads[group % 2][m - 1], device_id_type=MESH,
        )

    eset, lset = (e_snd, e_all, e_ss, e_rs), (l_snd, l_all, l_ss, l_rs)
    cset = (c_snd, c_all, c_ss, c_rs)

    def take(group, kind, buf):
        for slot in range(4 * group + 3, 4 * group - 1, -1):
            if slot:
                arrival(slot, *kind).wait_recv()
        turned = dot(perm[...], kind[1][rows(group, GROUP), :]).astype(BF16)
        for b in range(BLOCKS):
            buf[rows(group, MSG), b * CUT:(b + 1) * CUT] = turned[b * MSG:(b + 1) * MSG, :]

    def spill(half, classes, values, kind):
        low = 256 if classes else 0
        for m in (3, 2, 1, 0):
            buf = kind[0] if m else kind[1]
            place = pl.ds(GROUP * (m - 1) + half * HALF if m else 4 * half * HALF, HALF)
            if classes:
                buf[place, 0:128] = classes[m][0]
                buf[place, 128:256] = classes[m][1]
            for i, value in enumerate(values):
                buf[place, low + i * 384:low + (i + 1) * 384] = value
            if m:
                for group in (2 * half + 1, 2 * half):
                    forward(group, m, *kind).start()

    def early(half):
        at = rows(half, HALF)
        pre = dot(xs[at, :], gu[...])
        a, u = pre[:, :384], pre[:, 384:]
        s = 1.0 / (1.0 + jnp.exp(-a))
        silu = a * s
        p1[at, :] = u * s * (1.0 + a * (1.0 - s))
        p2[at, :] = silu
        spill(half, pack(xs, at), [(silu * u).astype(BF16)], eset)

    def late(half):
        at = rows(half, HALF)
        spill(half, pack(gs, at), [], cset)
        d_act = dot(gs[at, :], down[...], NT)
        spill(half, None, [(d_act * p1[at, :]).astype(BF16), (d_act * p2[at, :]).astype(BF16)], lset)

    def give(value, kind):
        buf = kind[0]
        for group in ORDER:
            stacked = jnp.concatenate(
                [value[group * MSG:(group + 1) * MSG, b * CUT:(b + 1) * CUT] for b in range(BLOCKS)], axis=0
            )
            buf[rows(group, GROUP), :] = dot(perm[...], stacked).astype(BF16)
            for slot in range(4 * group + 3, 4 * group - 1, -1):
                if slot:
                    exchange(slot, *kind).start()

    def mine(buf, low, high):
        return jnp.concatenate([buf[rows(4 * half, HALF), low:high] for half in range(2)], axis=0)

    take(3, tset, xs)
    take(2, tset, xs)
    loads[10].wait()
    loads[11].wait()
    early(1)
    take(1, tset, xs)
    take(0, tset, xs)
    early(0)
    give(dot(mine(e_all, 256, 640), down[...]).astype(BF16), rset)
    pl.semaphore_wait(here.at[0], 1)
    pl.semaphore_wait(here.at[1], 1)
    tell(2, lax.rem(z + 2, 8))
    tell(3, lax.rem(z + 6, 8))
    take(3, gset, gs)
    take(2, gset, gs)
    late(1)
    pl.semaphore_wait(here.at[2], 1)
    pl.semaphore_wait(here.at[3], 1)
    tell(4, lax.rem(z + 4, 8))
    take(1, gset, gs)
    take(0, gset, gs)
    late(0)
    give(dot(mine(l_all, 0, 768), gu[...], NT).astype(BF16), dset)

    wset, vset = (part, got, w_ss, w_rs), (part_c, got_c, v_ss, v_rs)

    def share(m, src, dst, ss, rs):
        yy, zz = peer(m)
        other = ((4 - m // 4) % 4) * 4 + (4 - m % 4) % 4
        return pltpu.make_async_remote_copy(
            src.at[lax.div(zz, 2) * 4 + lax.div(yy, 2)], dst.at[other], ss.at[m], rs.at[other],
            device_id=dp_at(yy, zz), device_id_type=MESH,
        )

    def shared(m, src, dst, ss, rs):
        return pltpu.make_async_remote_copy(
            src.at[m], dst.at[m], ss.at[m], rs.at[m],
            device_id=dp_at(*peer(m)), device_id_type=MESH,
        )

    def made_of(kinds, left, right):
        product = 0.0
        for half in (1, 0):
            for m in (1, 2, 3):
                for group in (2 * half + 1, 2 * half):
                    for kind in kinds:
                        forward(group, m, *kind).wait_recv()
            at = rows(half, 4 * HALF)
            product = product + dot(left(at), right(at), TN)
        return product

    def send_blocks(product, kind, kept):
        for k in range(16):
            kind[0][k] = product[k * 16:(k + 1) * 16, :].astype(BF16)
        for m in PEERS:
            share(m, *kind).start()
        for k in range(16):
            kept[k] = product[k * 16:(k + 1) * 16, :]

    last = made_of((eset, cset), lambda at: c_all[at, :], lambda at: e_all[at, 256:640])
    pl.semaphore_wait(here.at[4], 1)
    send_blocks(last, vset, own_c)
    first = made_of((lset,), lambda at: e_all[at, 0:256], lambda at: l_all[at, :])
    send_blocks(first, wset, own)

    ret_r[0:MSG, :] = out_r[0:MSG, :]
    ret_d[0:MSG, :] = out_d[0:MSG, :]
    for slot in range(1, 16):
        arrival(slot, *rset).wait_recv()
    inner = jnp.zeros((128, 1), F32)
    for b in range(BLOCKS):
        copy_out = dot(gather[rows(b, 128), :], ret_r[...])
        mixed_ref[:, b * CUT:(b + 1) * CUT] = (weight * copy_out).astype(BF16)
        inner = inner + jnp.sum(grad[rows(b, 128), :].astype(F32) * copy_out, axis=1, keepdims=True)
    rwg_ref[...] = jnp.sum(jnp.where(eye, inner, 0.0), axis=0, keepdims=True)
    for slot in range(1, 16):
        arrival(slot, *dset).wait_recv()
    for b in range(BLOCKS):
        tgrad_ref[:, b * CUT:(b + 1) * CUT] = dot(gather[rows(b, 128), :], ret_d[...]).astype(BF16)

    mine_at = lax.div(z, 2) * 4 + lax.div(y, 2)
    for kind, kept, low, high in ((vset, own_c, 768, 1152), (wset, own, 0, 768)):
        total = kept[mine_at]
        for m in range(1, 16):
            shared(m, *kind).wait_recv()
            total = total + kind[1][m].astype(F32)
        wgrad_ref[0, :, low:high] = total

    for slot in range(1, 16):
        for kind in (tset, gset, rset, dset):
            exchange(slot, *kind).wait_send()
        share(slot, *vset).wait_send()
        share(slot, *wset).wait_send()
    for group in range(4):
        for m in (1, 2, 3):
            for kind in (eset, cset, lset):
                forward(group, m, *kind).wait_send()


def hand_over(*refs):
    taken, given, sem = refs[:4], refs[4:8], refs[8]
    copies = [pltpu.make_async_copy(a, b, sem.at[i]) for i, (a, b) in enumerate(zip(taken, given))]
    for copy in copies:
        copy.start()
    for copy in copies:
        copy.wait()


def on_device(tokens, route_ids, route_weight, w_gate_up, w_down, out_grad):
    count, width = tokens.shape
    hidden = w_down.shape[1]
    dma = pltpu.SemaphoreType.DMA
    vmem = pl.BlockSpec(memory_space=pltpu.VMEM)
    hbm = pl.BlockSpec(memory_space=pl.ANY)
    slots = 16 * MSG
    scratch = [
        pltpu.VMEM((1, count), I32), pltpu.VMEM((1, count), F32),
        pltpu.VMEM((512, CUT), BF16), pltpu.VMEM((512, CUT), BF16),
        pltpu.VMEM((width, 2 * hidden), BF16), pltpu.VMEM((hidden, width), BF16),
        pltpu.VMEM((slots, 512), BF16), pltpu.VMEM((512, slots), BF16), pltpu.VMEM((GROUP, GROUP), BF16),
        pltpu.VMEM((2, 256, 128), BF16),
        *[pltpu.VMEM((slots, CUT), BF16)] * 4,
        pltpu.VMEM((GROUP, width), BF16), pltpu.VMEM((GROUP, width), BF16),
        pltpu.VMEM((GROUP, hidden), F32), pltpu.VMEM((GROUP, hidden), F32),
        pltpu.VMEM((3 * GROUP, 256 + hidden), BF16), pltpu.VMEM((4 * GROUP, 256 + hidden), BF16),
        pltpu.VMEM((3 * GROUP, 256), BF16), pltpu.VMEM((4 * GROUP, 256), BF16),
        pltpu.VMEM((3 * GROUP, 2 * hidden), BF16), pltpu.VMEM((4 * GROUP, 2 * hidden), BF16),
        *[pltpu.VMEM((slots, CUT), BF16)] * 4,
        pltpu.VMEM((16, 16, 2 * hidden), BF16), pltpu.VMEM((16, 16, 2 * hidden), F32),
        pltpu.VMEM((16, 16, 2 * hidden), BF16),
        pltpu.VMEM((16, 16, hidden), BF16), pltpu.VMEM((16, 16, hidden), F32),
        pltpu.VMEM((16, 16, hidden), BF16),
        dma((12,)), *[dma((16,))] * 18,
        pltpu.SemaphoreType.REGULAR((5,)),
    ]
    outs = (
        jax.ShapeDtypeStruct((count, width), BF16),
        jax.ShapeDtypeStruct((count, width), BF16),
        jax.ShapeDtypeStruct((1, count), F32),
        jax.ShapeDtypeStruct((1, 16, 3 * hidden), F32),
    )
    made = pl.pallas_call(
        kernel,
        out_shape=tuple(pltpu.VMEM(o.shape, o.dtype) for o in outs),
        in_specs=[hbm] * 6,
        out_specs=[vmem] * 4,
        scratch_shapes=scratch,
        compiler_params=pltpu.CompilerParams(
            collective_id=0, has_side_effects=True, vmem_limit_bytes=58 * 2**20
        ),
    )(route_ids.reshape(1, count), route_weight.reshape(1, count), tokens, out_grad, w_gate_up, w_down)
    mixed, tgrad, rwg, wgrad = pl.pallas_call(
        hand_over,
        out_shape=outs,
        in_specs=[vmem] * 4,
        out_specs=[hbm] * 4,
        scratch_shapes=[dma((4,))],
        compiler_params=pltpu.CompilerParams(vmem_limit_bytes=2**21),
    )(*made)
    return mixed, tgrad, rwg.reshape(count, 1), wgrad


def solution(mesh):
    rows_split = P(("dp", "expert"), None)
    return jax.shard_map(
        on_device,
        mesh=mesh,
        in_specs=(rows_split, rows_split, rows_split, P("expert", None, None), P("expert", None, None), rows_split),
        out_specs=(rows_split, rows_split, rows_split, P("expert", "dp", None)),
        check_vma=False,
    )
```

```python
import jax
import jax.numpy as jnp
from jax import lax
from jax.experimental import pallas as pl
from jax.experimental.pallas import tpu as pltpu
from jax.sharding import PartitionSpec as P

MESH = pl.DeviceIdType.MESH
BF16, F32, I32 = jnp.bfloat16, jnp.float32, jnp.int32
CAP = 12
BLOCKS = 4
CUT = 256
MSG = CAP * BLOCKS
GROUP = 4 * MSG
CHIPS = (0, 1, 7, 2, 6, 3, 5, 4)
PLACE = {k: i for i, k in enumerate(CHIPS)}
FAR_FIRST = (14, 15, 12, 13, 10, 11, 8, 9, 6, 7, 4, 5, 2, 3, 1)
ORDER = (3, 2, 1, 0)
PEERS = (10, 9, 11, 6, 14, 5, 7, 13, 15, 8, 2, 1, 3, 4, 12)
HALF = 2 * MSG
NT = (((1,), (1,)), ((), ()))
TN = (((0,), (0,)), ((), ()))


def mirror(slot):
    return 2 * PLACE[(8 - CHIPS[slot // 2]) % 8] + slot % 2


def rows(at, n):
    return pl.ds(at * n, n)


def dot(a, b, dims=(((1,), (0,)), ((), ()))):
    return lax.dot_general(a, b, dims, preferred_element_type=F32)


def kernel(
    ids_hbm, wt_hbm, tok_hbm, grad_hbm, gu_hbm, down_hbm,
    mixed_ref, tgrad_ref, rwg_ref, wgrad_ref,
    ids_ref, wt_ref, tok, grad, gu, down, spread, gather, perm, picks,
    snd_t, snd_g, rcv_t, rcv_g, xs, gs, p1, p2, e_snd, e_all, c_snd, c_all, l_snd, l_all,
    out_r, out_d, ret_r, ret_d, part, own, got, part_c, own_c, got_c,
    ld_sem, t_ss, t_rs, g_ss, g_rs, r_ss, r_rs, d_ss, d_rs,
    e_ss, e_rs, l_ss, l_rs, w_ss, w_rs, c_ss, c_rs, v_ss, v_rs, here,
):
    dp, ex = lax.axis_index("dp"), lax.axis_index("expert")
    y, z = lax.rem(dp, 8), lax.div(dp, 8)
    x, core = lax.div(ex, 2), lax.rem(ex, 2)

    def expert_at(slot):
        chip = lax.rem(x + CHIPS[slot // 2], 8)
        return {"expert": chip * 2 + (core if slot % 2 == 0 else 1 - core)}

    def dp_at(yy, zz):
        return {"dp": zz * 8 + yy}

    y0, z0 = y + 1 - 2 * lax.rem(y, 2), z + 1 - 2 * lax.rem(z, 2)
    y1, z1 = lax.rem(y + 7 + 2 * lax.rem(y, 2), 8), lax.rem(z + 7 + 2 * lax.rem(z, 2), 8)
    quads = (
        (dp_at(y0, z), dp_at(y, z0), dp_at(y0, z0)),
        (dp_at(y1, z), dp_at(y, z1), dp_at(y1, z1)),
    )

    def peer(m):
        return lax.rem(y + 2 * (m % 4), 8), lax.rem(z + 2 * (m // 4), 8)

    loads = [
        pltpu.make_async_copy(ids_hbm, ids_ref, ld_sem.at[10]),
        pltpu.make_async_copy(wt_hbm, wt_ref, ld_sem.at[11]),
    ]
    for b in range(BLOCKS):
        loads.append(pltpu.make_async_copy(tok_hbm.at[:, rows(b, CUT)], tok.at[rows(b, 128)], ld_sem.at[b]))
    for b in range(BLOCKS):
        loads.append(pltpu.make_async_copy(grad_hbm.at[:, rows(b, CUT)], grad.at[rows(b, 128)], ld_sem.at[4 + b]))
    loads.append(pltpu.make_async_copy(gu_hbm.at[0], gu, ld_sem.at[8]))
    loads.append(pltpu.make_async_copy(down_hbm.at[0], down, ld_sem.at[9]))

    barrier = pltpu.get_barrier_semaphore()
    for load in loads[:2]:
        load.start()
    for slot in FAR_FIRST:
        pl.semaphore_signal(barrier, 1, device_id=expert_at(slot), device_id_type=MESH)
    for m in (2, 1, 3):
        pl.semaphore_signal(barrier, 1, device_id=dp_at(*peer(m)), device_id_type=MESH)
    for quad in quads:
        for device in quad:
            pl.semaphore_signal(barrier, 1, device_id=device, device_id_type=MESH)
    for load in loads[2:]:
        load.start()

    sub = lax.broadcasted_iota(I32, (128, 128), 0)
    lane = lax.broadcasted_iota(I32, (128, 128), 1)
    eye = sub == lane

    def column(row):
        return jnp.sum(jnp.where(eye, row, 0.0), axis=1, keepdims=True)

    loads[0].wait()
    loads[1].wait()
    ids = ids_ref[...]
    chip = ((ids >> 1) + (8 - x)) & 7
    place = jnp.where(chip > 4, 16 - 2 * chip, jnp.where(chip == 0, 0, 2 * chip - 1))
    slot_row = (2 * place + ((ids + core) & 1)).astype(F32)
    slot_col = column(slot_row)
    same = slot_row == slot_col
    before_row = jnp.sum(jnp.where(same & (sub < lane), 1.0, 0.0), axis=0, keepdims=True)
    before_col = jnp.sum(jnp.where(same & (lane < sub), 1.0, 0.0), axis=1, keepdims=True)
    at_row = (slot_row * float(MSG) + before_row).astype(I32)
    at_col = (slot_col * float(MSG) + before_col).astype(I32)
    weight = column(wt_ref[...])

    down_rows = lax.broadcasted_iota(I32, (16 * MSG, 128), 0)
    for b in range(BLOCKS):
        spread[:, b * 128:(b + 1) * 128] = jnp.where(down_rows == at_row + CAP * b, 1.0, 0.0).astype(BF16)
    for b in range(BLOCKS):
        loads[2 + b].wait()
    snd_t[...] = dot(spread[...], tok[...]).astype(BF16)

    pl.semaphore_wait(barrier, 24)

    def exchange(slot, src, dst, ss, rs):
        other = mirror(slot)
        return pltpu.make_async_remote_copy(
            src.at[rows(slot, MSG)], dst.at[rows(other, MSG)], ss.at[slot], rs.at[other],
            device_id=expert_at(slot), device_id_type=MESH,
        )

    def arrival(slot, src, dst, ss, rs):
        return pltpu.make_async_remote_copy(
            src.at[rows(slot, MSG)], dst.at[rows(slot, MSG)], ss.at[slot], rs.at[slot],
            device_id=expert_at(slot), device_id_type=MESH,
        )

    tset, gset = (snd_t, rcv_t, t_ss, t_rs), (snd_g, rcv_g, g_ss, g_rs)
    rset, dset = (out_r, ret_r, r_ss, r_rs), (out_d, ret_d, d_ss, d_rs)
    for slot in FAR_FIRST:
        exchange(slot, *tset).start()
    for b in range(BLOCKS):
        loads[6 + b].wait()
    for b in range(BLOCKS):
        grad_b = grad[rows(b, 128), :].astype(F32)
        tok[rows(b, 128), :] = (weight * grad_b).astype(BF16)
    snd_g[...] = dot(spread[...], tok[...]).astype(BF16)
    for slot in FAR_FIRST:
        exchange(slot, *gset).start()

    def tell(i, zz):
        pl.semaphore_signal(here.at[i], 1, device_id=dp_at(y, zz), device_id_type=MESH)

    tell(0, z0)
    tell(1, z1)
    rcv_t[0:MSG, :] = snd_t[0:MSG, :]
    rcv_g[0:MSG, :] = snd_g[0:MSG, :]

    up = lax.broadcasted_iota(I32, (GROUP, GROUP), 0)
    across = lax.broadcasted_iota(I32, (GROUP, GROUP), 1)
    twelfth = (up * 5462) >> 16
    target = (twelfth & 3) * MSG + (twelfth >> 2) * CAP + (up - twelfth * CAP)
    perm[...] = jnp.where(across == target, 1.0, 0.0).astype(BF16)
    for b in range(BLOCKS):
        right = lax.broadcasted_iota(I32, (128, 16 * MSG), 1)
        gather[rows(b, 128), :] = jnp.where(right == at_col + CAP * b, 1.0, 0.0).astype(BF16)

    lanes_in = lax.broadcasted_iota(I32, (256, 128), 0)
    lanes_out = lax.broadcasted_iota(I32, (256, 128), 1)
    goal = (lanes_in >> 7) * 64 + ((lanes_in >> 5) & 3) * 16 + (lanes_in & 15)
    odd_y, odd_z = lax.rem(y, 2), lax.rem(z, 2)
    for flip in range(2):
        parity = odd_y if flip == 0 else 1 - odd_y
        picks[flip] = jnp.where((lanes_out == goal) & (((lanes_in >> 4) & 1) == parity), 1.0, 0.0).astype(BF16)

    def pack(buf, at):
        classes = [None] * 4
        for flip in range(2):
            pieces = []
            for odd in (odd_z, 1 - odd_z):
                for h in range(2):
                    left = pl.ds(pl.multiple_of((odd + 4 * h) * 128, 128), 128)
                    right = pl.ds(pl.multiple_of((odd + 4 * h + 2) * 128, 128), 128)
                    pieces.append(jnp.concatenate([buf[at, left], buf[at, right]], axis=1))
            chosen = dot(jnp.concatenate(pieces, axis=0), picks[flip]).astype(BF16)
            for k in range(2):
                classes[flip + 2 * k] = (
                    chosen[2 * k * HALF:(2 * k + 1) * HALF, :], chosen[(2 * k + 1) * HALF:(2 * k + 2) * HALF, :]
                )
        return classes

    def spot(m, group):
        return (group // 2) * 8 + 2 * m + group % 2

    def forward(group, m, src, dst, ss, rs):
        return pltpu.make_async_remote_copy(
            src.at[rows(4 * (m - 1) + group, MSG)], dst.at[rows(spot(m, group), MSG)],
            ss.at[4 * m + group], rs.at[4 * m + group],
            device_id=quads[group % 2][m - 1], device_id_type=MESH,
        )

    eset, lset = (e_snd, e_all, e_ss, e_rs), (l_snd, l_all, l_ss, l_rs)
    cset = (c_snd, c_all, c_ss, c_rs)

    def take(group, kind, buf):
        for slot in range(4 * group + 3, 4 * group - 1, -1):
            if slot:
                arrival(slot, *kind).wait_recv()
        turned = dot(perm[...], kind[1][rows(group, GROUP), :]).astype(BF16)
        for b in range(BLOCKS):
            buf[rows(group, MSG), b * CUT:(b + 1) * CUT] = turned[b * MSG:(b + 1) * MSG, :]

    def spill(half, classes, values, kind):
        low = 256 if classes else 0
        for m in (3, 2, 1, 0):
            buf = kind[0] if m else kind[1]
            place = pl.ds(GROUP * (m - 1) + half * HALF if m else 4 * half * HALF, HALF)
            if classes:
                buf[place, 0:128] = classes[m][0]
                buf[place, 128:256] = classes[m][1]
            for i, value in enumerate(values):
                buf[place, low + i * 384:low + (i + 1) * 384] = value
            if m:
                for group in (2 * half + 1, 2 * half):
                    forward(group, m, *kind).start()

    def early(half):
        at = rows(half, HALF)
        pre = dot(xs[at, :], gu[...])
        a, u = pre[:, :384], pre[:, 384:]
        s = 1.0 / (1.0 + jnp.exp(-a))
        silu = a * s
        p1[at, :] = u * s * (1.0 + a * (1.0 - s))
        p2[at, :] = silu
        spill(half, pack(xs, at), [(silu * u).astype(BF16)], eset)

    def late(half):
        at = rows(half, HALF)
        spill(half, pack(gs, at), [], cset)
        d_act = dot(gs[at, :], down[...], NT)
        spill(half, None, [(d_act * p1[at, :]).astype(BF16), (d_act * p2[at, :]).astype(BF16)], lset)

    def give(value, kind):
        buf = kind[0]
        for group in ORDER:
            stacked = jnp.concatenate(
                [value[group * MSG:(group + 1) * MSG, b * CUT:(b + 1) * CUT] for b in range(BLOCKS)], axis=0
            )
            buf[rows(group, GROUP), :] = dot(perm[...], stacked).astype(BF16)
            for slot in range(4 * group + 3, 4 * group - 1, -1):
                if slot:
                    exchange(slot, *kind).start()

    def mine(buf, low, high):
        return jnp.concatenate([buf[rows(4 * half, HALF), low:high] for half in range(2)], axis=0)

    take(3, tset, xs)
    take(2, tset, xs)
    loads[10].wait()
    loads[11].wait()
    early(1)
    take(1, tset, xs)
    take(0, tset, xs)
    early(0)
    give(dot(mine(e_all, 256, 640), down[...]).astype(BF16), rset)
    pl.semaphore_wait(here.at[0], 1)
    pl.semaphore_wait(here.at[1], 1)
    tell(2, lax.rem(z + 2, 8))
    tell(3, lax.rem(z + 6, 8))
    take(3, gset, gs)
    take(2, gset, gs)
    late(1)
    pl.semaphore_wait(here.at[2], 1)
    pl.semaphore_wait(here.at[3], 1)
    tell(4, lax.rem(z + 4, 8))
    take(1, gset, gs)
    take(0, gset, gs)
    late(0)
    give(dot(mine(l_all, 0, 768), gu[...], NT).astype(BF16), dset)

    wset, vset = (part, got, w_ss, w_rs), (part_c, got_c, v_ss, v_rs)

    def share(m, src, dst, ss, rs):
        yy, zz = peer(m)
        other = ((4 - m // 4) % 4) * 4 + (4 - m % 4) % 4
        return pltpu.make_async_remote_copy(
            src.at[lax.div(zz, 2) * 4 + lax.div(yy, 2)], dst.at[other], ss.at[m], rs.at[other],
            device_id=dp_at(yy, zz), device_id_type=MESH,
        )

    def shared(m, src, dst, ss, rs):
        return pltpu.make_async_remote_copy(
            src.at[m], dst.at[m], ss.at[m], rs.at[m],
            device_id=dp_at(*peer(m)), device_id_type=MESH,
        )

    def made_of(kinds, left, right):
        product = 0.0
        for half in (1, 0):
            for m in (1, 2, 3):
                for group in (2 * half + 1, 2 * half):
                    for kind in kinds:
                        forward(group, m, *kind).wait_recv()
            at = rows(half, 4 * HALF)
            product = product + dot(left(at), right(at), TN)
        return product

    def send_blocks(product, kind, kept):
        for k in range(16):
            kind[0][k] = product[k * 16:(k + 1) * 16, :].astype(BF16)
        for m in PEERS:
            share(m, *kind).start()
        for k in range(16):
            kept[k] = product[k * 16:(k + 1) * 16, :]

    last = made_of((eset, cset), lambda at: c_all[at, :], lambda at: e_all[at, 256:640])
    pl.semaphore_wait(here.at[4], 1)
    send_blocks(last, vset, own_c)
    first = made_of((lset,), lambda at: e_all[at, 0:256], lambda at: l_all[at, :])
    send_blocks(first, wset, own)

    ret_r[0:MSG, :] = out_r[0:MSG, :]
    ret_d[0:MSG, :] = out_d[0:MSG, :]
    for slot in range(1, 16):
        arrival(slot, *rset).wait_recv()
    inner = jnp.zeros((128, 1), F32)
    for b in range(BLOCKS):
        copy_out = dot(gather[rows(b, 128), :], ret_r[...])
        mixed_ref[:, b * CUT:(b + 1) * CUT] = (weight * copy_out).astype(BF16)
        inner = inner + jnp.sum(grad[rows(b, 128), :].astype(F32) * copy_out, axis=1, keepdims=True)
    rwg_ref[...] = jnp.sum(jnp.where(eye, inner, 0.0), axis=0, keepdims=True)
    for slot in range(1, 16):
        arrival(slot, *dset).wait_recv()
    for b in range(BLOCKS):
        tgrad_ref[:, b * CUT:(b + 1) * CUT] = dot(gather[rows(b, 128), :], ret_d[...]).astype(BF16)

    for slot in range(1, 16):
        for kind in (tset, gset, rset, dset):
            exchange(slot, *kind).wait_send()
    for group in range(4):
        for m in (1, 2, 3):
            for kind in (eset, cset, lset):
                forward(group, m, *kind).wait_send()
    for slot in range(1, 16):
        share(slot, *vset).wait_send()

    mine_at = lax.div(z, 2) * 4 + lax.div(y, 2)
    for kind, kept, low, high in ((vset, own_c, 768, 1152), (wset, own, 0, 768)):
        total = kept[mine_at]
        if kind is wset:
            for m in range(1, 16):
                share(m, *wset).wait_send()
        for m in range(1, 16):
            shared(m, *kind).wait_recv()
            total = total + kind[1][m].astype(F32)
        wgrad_ref[0, :, low:high] = total


def hand_over(*refs):
    taken, given, sem = refs[:4], refs[4:8], refs[8]
    copies = [pltpu.make_async_copy(a, b, sem.at[i]) for i, (a, b) in enumerate(zip(taken, given))]
    for copy in copies:
        copy.start()
    for copy in copies:
        copy.wait()


def on_device(tokens, route_ids, route_weight, w_gate_up, w_down, out_grad):
    count, width = tokens.shape
    hidden = w_down.shape[1]
    dma = pltpu.SemaphoreType.DMA
    vmem = pl.BlockSpec(memory_space=pltpu.VMEM)
    hbm = pl.BlockSpec(memory_space=pl.ANY)
    slots = 16 * MSG
    scratch = [
        pltpu.VMEM((1, count), I32), pltpu.VMEM((1, count), F32),
        pltpu.VMEM((512, CUT), BF16), pltpu.VMEM((512, CUT), BF16),
        pltpu.VMEM((width, 2 * hidden), BF16), pltpu.VMEM((hidden, width), BF16),
        pltpu.VMEM((slots, 512), BF16), pltpu.VMEM((512, slots), BF16), pltpu.VMEM((GROUP, GROUP), BF16),
        pltpu.VMEM((2, 256, 128), BF16),
        *[pltpu.VMEM((slots, CUT), BF16)] * 4,
        pltpu.VMEM((GROUP, width), BF16), pltpu.VMEM((GROUP, width), BF16),
        pltpu.VMEM((GROUP, hidden), F32), pltpu.VMEM((GROUP, hidden), F32),
        pltpu.VMEM((3 * GROUP, 256 + hidden), BF16), pltpu.VMEM((4 * GROUP, 256 + hidden), BF16),
        pltpu.VMEM((3 * GROUP, 256), BF16), pltpu.VMEM((4 * GROUP, 256), BF16),
        pltpu.VMEM((3 * GROUP, 2 * hidden), BF16), pltpu.VMEM((4 * GROUP, 2 * hidden), BF16),
        *[pltpu.VMEM((slots, CUT), BF16)] * 4,
        pltpu.VMEM((16, 16, 2 * hidden), BF16), pltpu.VMEM((16, 16, 2 * hidden), F32),
        pltpu.VMEM((16, 16, 2 * hidden), BF16),
        pltpu.VMEM((16, 16, hidden), BF16), pltpu.VMEM((16, 16, hidden), F32),
        pltpu.VMEM((16, 16, hidden), BF16),
        dma((12,)), *[dma((16,))] * 18,
        pltpu.SemaphoreType.REGULAR((5,)),
    ]
    outs = (
        jax.ShapeDtypeStruct((count, width), BF16),
        jax.ShapeDtypeStruct((count, width), BF16),
        jax.ShapeDtypeStruct((1, count), F32),
        jax.ShapeDtypeStruct((1, 16, 3 * hidden), F32),
    )
    made = pl.pallas_call(
        kernel,
        out_shape=tuple(pltpu.VMEM(o.shape, o.dtype) for o in outs),
        in_specs=[hbm] * 6,
        out_specs=[vmem] * 4,
        scratch_shapes=scratch,
        compiler_params=pltpu.CompilerParams(
            collective_id=0, has_side_effects=True, vmem_limit_bytes=58 * 2**20
        ),
    )(route_ids.reshape(1, count), route_weight.reshape(1, count), tokens, out_grad, w_gate_up, w_down)
    mixed, tgrad, rwg, wgrad = pl.pallas_call(
        hand_over,
        out_shape=outs,
        in_specs=[vmem] * 4,
        out_specs=[hbm] * 4,
        scratch_shapes=[dma((4,))],
        compiler_params=pltpu.CompilerParams(vmem_limit_bytes=2**21),
    )(*made)
    return mixed, tgrad, rwg.reshape(count, 1), wgrad


def solution(mesh):
    rows_split = P(("dp", "expert"), None)
    return jax.shard_map(
        on_device,
        mesh=mesh,
        in_specs=(rows_split, rows_split, rows_split, P("expert", None, None), P("expert", None, None), rows_split),
        out_specs=(rows_split, rows_split, rows_split, P("expert", "dp", None)),
        check_vma=False,
    )
```
